32 devices in a mesh: pw: 16 (over z, y, core), band: 2 (over x).
Axes of the slice: x: 2, y: 2, z: 4, core: 2. Of those that a mesh axis runs over, the one named last changes fastest.
Arguments:
- waves: bfloat16 [2, 20480, 1792], P(None, 'pw', 'band'), may hold values from -6 to 6
- projectors: bfloat16 [2, 128, 20480], P(None, 'band', 'pw'), may hold values from -0.03125 to 0.03125
- coupling: float32 [12, 13, 13], replicated, may hold values from -22.768398 to 22.768398
- offsets: int32 [12], replicated, may hold values from 0 to 119, as said below
- counts: int32 [12], replicated, may hold values from 9 to 13, as said below
Outputs:
- applied: bfloat16 [2, 20480, 1792], P(None, 'pw', 'band')
The draws below stay inside these ranges and needn't reach their ends.
Inputs may be any that keep to these rules, and one draw needn't show every extreme that they name: `counts`: each atom has 9 or 13 projectors, exactly 5 atoms have 13, so the atoms fill all 128 projectors. offsets are the running sums of counts before each atom, so atoms take consecutive projectors in order.
All inputs are finite; a program needn't handle non-finite values.
Results may differ from the reference program's by a relative error of at most 0.0049.
Values may be sent and summed in bfloat16 or wider, within the bound.
A program may use at most 64 MiB of HBM per device.

```python
import jax
import jax.numpy as jnp
from jax import lax

NB_DEV = 896
NP = 128
NATOM = 12
M = 13
NPW = 20480
NB = 1792
N_BAND = 2


def atom_sizes(key):
    order = jax.random.permutation(key, NATOM)
    return jnp.where(order < 5, 13, 9).astype(jnp.int32)


def draw_counts(key, part):
    return atom_sizes(key)


def draw_offsets(key, part):
    sizes = atom_sizes(key)
    return (jnp.cumsum(sizes) - sizes).astype(jnp.int32)


def steps_of(key, extent, cuts, low, largest):
    def one(position, parts):
        steps = jax.random.uniform(jax.random.fold_in(jax.random.fold_in(key, 6), position), (parts,), jnp.float32, low / len(cuts), largest / len(cuts))
        return jnp.repeat(jnp.exp(steps), extent[position] // parts).reshape((-1,) + (1,) * (len(extent) - position - 1))

    level = one(*cuts[0])
    for cut in cuts[1:]:
        level = level * one(*cut)
    return level


def scatter_about(key, extent, scale, reach, shards=(), held_as=jnp.bfloat16):
    array = jax.random.normal(key, extent, jnp.float32) * scale
    if len(shards) > 0:
        array = steps_of(key, extent, shards, -0.22, 0.18) * array
    return jnp.clip(array, min=-reach, max=reach).astype(held_as)


def setup_inputs(seed: int = 0) -> dict:
    key_list = jax.random.split(jax.random.key(seed), 6)
    return {
        "waves": scatter_about(key_list[0], (2, NPW, NB), 1.0, 6.0, ((1, 16), (2, 2))),
        "projectors": scatter_about(key_list[1], (2, NP, NPW), (2 * NPW) ** -0.5, 0.03125, ((1, 2), (2, 16))),
        "coupling": scatter_about(key_list[2], (NATOM, M, M), (0.3 * (NPW / NP) ** 0.5), 22.768398, (), jnp.float32),
        "offsets": draw_offsets(jax.random.fold_in(key_list[5], 71), 0),
        "counts": draw_counts(jax.random.fold_in(key_list[5], 71), 0),
    }


def coupling_block(coupling, offsets, counts):
    proj = jnp.arange(NP, dtype=jnp.int32)
    local = jnp.arange(M, dtype=jnp.int32)
    target = offsets[:, None] + local[None, :]
    select = (proj[None, :, None] == target[:, None, :]) & (local[None, None, :] < counts[:, None, None])
    select = select.astype(jnp.float32)
    sym = (coupling + jnp.swapaxes(coupling, 1, 2)) * 0.5
    return jnp.einsum('api,aij,aqj->pq', select, sym, select, precision=lax.Precision.HIGHEST)


def reference(waves, projectors, coupling, offsets, counts):
    block = coupling_block(coupling, offsets, counts)

    def one_block(index):
        start = (index * NB_DEV).astype(jnp.int32)
        part = lax.dynamic_slice_in_dim(waves, start, NB_DEV, 2)
        real = jnp.dot(projectors[0], part[0], preferred_element_type=jnp.float32) + jnp.dot(projectors[1], part[1], preferred_element_type=jnp.float32)
        imag = jnp.dot(projectors[0], part[1], preferred_element_type=jnp.float32) - jnp.dot(projectors[1], part[0], preferred_element_type=jnp.float32)
        coeffs = jnp.stack([real, imag])
        coupled = jnp.einsum('pq,kqb->kpb', block, coeffs, precision=lax.Precision.HIGHEST).astype(jnp.bfloat16)
        dims = (((0,), (0,)), ((), ()))
        out_real = lax.dot_general(projectors[0], coupled[0], dims, preferred_element_type=jnp.float32) - lax.dot_general(projectors[1], coupled[1], dims, preferred_element_type=jnp.float32)
        out_imag = lax.dot_general(projectors[0], coupled[1], dims, preferred_element_type=jnp.float32) + lax.dot_general(projectors[1], coupled[0], dims, preferred_element_type=jnp.float32)
        return jnp.stack([out_real, out_imag]).astype(jnp.bfloat16)

    blocks = lax.map(one_block, jnp.arange(N_BAND, dtype=jnp.int32))
    return jnp.transpose(blocks, (1, 2, 0, 3)).reshape(2, NPW, NB)
```

```python
import functools

import jax
import jax.numpy as jnp
from jax import lax
from jax.experimental import pallas as pl
from jax.experimental.pallas import tpu as pltpu
from jax.sharding import PartitionSpec as P

NP = 128
M = 13
LANES = 128
MESH = pl.DeviceIdType.MESH


def coupling_block(coupling, offsets, counts):
    proj = jnp.arange(NP, dtype=jnp.int32)
    local = jnp.arange(M, dtype=jnp.int32)
    target = offsets[:, None] + local[None, :]
    select = (proj[None, :, None] == target[:, None, :]) & (
        local[None, None, :] < counts[:, None, None]
    )
    select = select.astype(jnp.float32)
    sym = (coupling + jnp.swapaxes(coupling, 1, 2)) * 0.5
    return jnp.einsum("api,aij,aqj->pq", select, sym, select, precision=lax.Precision.HIGHEST)


def column_tiles(columns):
    return [(start, min(256, columns - start)) for start in range(0, columns, 256)]


def gather_kernel(n_pw, n_band, waves, proj, block, pt_out, c_out,
                  w, p_all, acc, sib, send, recv, total, c_all, pt,
                  w_sem, own_sem, out_sem, p_send, p_recv, s_send, s_recv,
                  r_send, r_recv, g_send, g_recv, f_send, f_recv):
    pw = lax.axis_index("pw")
    band = lax.axis_index("band")
    chip, core = lax.div(pw, 2), lax.rem(pw, 2)
    chips = n_pw // 2
    held = proj.shape[1]
    columns = waves.shape[2]
    blocks = columns // LANES
    piece = min(32, held)
    tiles = column_tiles(columns)
    sibling = (chip * 2 + 1 - core, band)

    def chip_at(step):
        return lax.rem(chip + step, chips)

    def same_core(other):
        return (other * 2 + core, band)

    wave_copies = []
    for t, (start, size) in enumerate(tiles):
        copy = pltpu.make_async_copy(
            waves.at[:, :, pl.ds(start, size)], w.at[:, :, pl.ds(start, size)], w_sem.at[t])
        copy.start()
        wave_copies.append(copy)
    own_rows = pl.multiple_of(band * held, held)
    own = pltpu.make_async_copy(proj, p_all.at[:, pl.ds(own_rows, held), :], own_sem.at[0])
    own.start()

    barrier = pltpu.get_barrier_semaphore()
    for d in range(1, n_band):
        pl.semaphore_signal(barrier, inc=1, device_id=(pw, lax.rem(band + d, n_band)), device_id_type=MESH)
    pl.semaphore_signal(barrier, inc=1, device_id=sibling, device_id_type=MESH)
    for d in range(1, chips):
        pl.semaphore_signal(barrier, inc=1, device_id=same_core(chip_at(d)), device_id_type=MESH)
    pl.semaphore_wait(barrier, n_band - 1 + 1 + chips - 1)

    p_copies = {}
    for d in range(1, n_band):
        for s in range(held // piece):
            rows = pl.ds(pl.multiple_of(band * held + s * piece, piece), piece)
            copy = pltpu.make_async_remote_copy(
                src_ref=proj.at[:, pl.ds(s * piece, piece), :],
                dst_ref=p_all.at[:, rows, :],
                send_sem=p_send.at[d - 1, s], recv_sem=p_recv.at[d - 1, s],
                device_id=(pw, lax.rem(band + d, n_band)), device_id_type=MESH)
            copy.start()
            p_copies[d, s] = copy

    def project(row, size, first):
        rows = pl.ds(row, size)
        p0, p1 = p_all[0, rows, :], p_all[1, rows, :]
        lhs0 = jnp.concatenate([p0, -p1], axis=0)
        lhs1 = jnp.concatenate([p1, p0], axis=0)
        for t, (start, width) in enumerate(tiles):
            if first:
                wave_copies[t].wait()
            cols = pl.ds(start, width)
            r = jnp.dot(lhs0, w[0, :, cols], preferred_element_type=jnp.float32)
            r += jnp.dot(lhs1, w[1, :, cols], preferred_element_type=jnp.float32)
            acc[0, rows, cols] = r[:size]
            acc[1, rows, cols] = r[size:]

    sends = []

    def reduce_piece(i, row, size):
        rows = pl.ds(row, size)
        copy = pltpu.make_async_remote_copy(
            src_ref=acc.at[1 - core, rows, :], dst_ref=sib.at[rows, :],
            send_sem=s_send.at[i], recv_sem=s_recv.at[i],
            device_id=sibling, device_id_type=MESH)
        copy.start()
        copy.wait_recv()
        sends.append((None, copy))
        for b in range(blocks):
            cols = pl.ds(b * LANES, LANES)
            send[b, rows, :] = (acc[core, rows, cols] + sib[rows, cols]).astype(jnp.bfloat16)
        for d in range(1, chips):
            other = chip_at(d)

            @pl.when(other < blocks)
            def _():
                reduce_copy(i, d, row, size).start()
            sends.append((other < blocks, reduce_copy(i, d, row, size)))

    def reduce_copy(i, d, row, size):
        other = chip_at(d)
        return pltpu.make_async_remote_copy(
            src_ref=send.at[lax.min(other, blocks - 1), pl.ds(row, size), :],
            dst_ref=recv.at[chip, pl.ds(row, size), :],
            send_sem=r_send.at[i, d], recv_sem=r_recv.at[i, chip],
            device_id=same_core(other), device_id_type=MESH)

    pieces = [(own_rows, held)]
    own.wait()
    project(own_rows, held, True)
    reduce_piece(0, own_rows, held)
    for d in range(1, n_band):
        source = lax.rem(band + n_band - d, n_band)
        for s in range(held // piece):
            p_copies[d, s].wait_recv()
            row = pl.multiple_of(source * held + s * piece, piece)
            project(row, piece, False)
            reduce_piece(len(pieces), row, piece)
            pieces.append((row, piece))

    pt[:, :NP] = p_all[0].T
    pt[:, NP:] = p_all[1].T
    pt_copy = pltpu.make_async_copy(pt, pt_out, out_sem.at[0])
    pt_copy.start()

    def gather_copy(b, d):
        return pltpu.make_async_remote_copy(
            src_ref=c_all.at[core, b], dst_ref=c_all.at[core, b],
            send_sem=g_send.at[d], recv_sem=g_recv.at[b],
            device_id=same_core(chip_at(d)), device_id_type=MESH)

    def forward_copy(k, b):
        return pltpu.make_async_remote_copy(
            src_ref=c_all.at[k, b], dst_ref=c_all.at[k, b],
            send_sem=f_send.at[b], recv_sem=f_recv.at[b],
            device_id=sibling, device_id_type=MESH)

    @pl.when(chip < blocks)
    def _():
        for i, (row, size) in enumerate(pieces):
            rows = pl.ds(row, size)
            value = send[chip, rows, :].astype(jnp.float32)
            for d in range(1, chips):
                source = chip_at(d)
                pltpu.make_async_remote_copy(
                    src_ref=send.at[0, rows, :], dst_ref=recv.at[source, rows, :],
                    send_sem=r_send.at[i, d], recv_sem=r_recv.at[i, source],
                    device_id=same_core(source), device_id_type=MESH).wait_recv()
                value += recv[source, rows, :].astype(jnp.float32)
            total[rows, :] = value
        c_all[core, chip] = jnp.dot(
            block[...], total[...], precision=lax.Precision.HIGHEST,
            preferred_element_type=jnp.float32).astype(jnp.bfloat16)
        for d in range(1, chips):
            gather_copy(chip, d).start()
        forward_copy(core, chip).start()

    for d in range(1, chips):
        source = chip_at(d)

        @pl.when(source < blocks)
        def _():
            gather_copy(source, d).wait_recv()
            forward_copy(core, source).start()

    for b in range(blocks):
        forward_copy(1 - core, b).wait_recv()
    c_copy = pltpu.make_async_copy(c_all, c_out, out_sem.at[1])
    c_copy.start()

    for copy in p_copies.values():
        copy.wait_send()
    for wanted, copy in sends:
        if wanted is None:
            copy.wait_send()
        else:
            pl.when(wanted)(copy.wait_send)

    @pl.when(chip < blocks)
    def _():
        for d in range(1, chips):
            gather_copy(chip, d).wait_send()
    for b in range(blocks):
        forward_copy(core, b).wait_send()
    pt_copy.wait()
    c_copy.wait()


def gather_coupled(n_pw, n_band, waves, projectors, block):
    _, depth, columns = waves.shape
    held = projectors.shape[1]
    chips = n_pw // 2
    blocks = columns // LANES
    subs = held // min(32, held)
    pieces = 1 + (n_band - 1) * subs
    bf16, f32 = jnp.bfloat16, jnp.float32
    dma = pltpu.SemaphoreType.DMA
    hbm = pl.BlockSpec(memory_space=pl.ANY)
    return pl.pallas_call(
        functools.partial(gather_kernel, n_pw, n_band),
        out_shape=[
            jax.ShapeDtypeStruct((depth, 2 * NP), bf16),
            jax.ShapeDtypeStruct((2, blocks, NP, LANES), bf16),
        ],
        in_specs=[hbm, hbm, pl.BlockSpec(memory_space=pltpu.VMEM)],
        out_specs=[hbm, hbm],
        scratch_shapes=[
            pltpu.VMEM((2, depth, columns), bf16),
            pltpu.VMEM((2, NP, depth), bf16),
            pltpu.VMEM((2, NP, columns), f32),
            pltpu.VMEM((NP, columns), f32),
            pltpu.VMEM((blocks, NP, LANES), bf16),
            pltpu.VMEM((chips, NP, LANES), bf16),
            pltpu.VMEM((NP, LANES), f32),
            pltpu.VMEM((2, blocks, NP, LANES), bf16),
            pltpu.VMEM((depth, 2 * NP), bf16),
            dma((len(column_tiles(columns)),)), dma((1,)), dma((2,)),
            dma((n_band - 1, subs)), dma((n_band - 1, subs)),
            dma((pieces,)), dma((pieces,)),
            dma((pieces, chips)), dma((pieces, chips)),
            dma((chips,)), dma((blocks,)),
            dma((blocks,)), dma((blocks,)),
        ],
        compiler_params=pltpu.CompilerParams(
            collective_id=0, has_side_effects=True, vmem_limit_bytes=40 * 2**20),
        name="gather_coupled",
    )(waves, projectors, block)


def spread_kernel(pt, c, out):
    c0, c1 = c[0, 0], c[1, 0]
    rhs = jnp.concatenate(
        [jnp.concatenate([c0, c1], axis=1), jnp.concatenate([-c1, c0], axis=1)], axis=0)
    r = jnp.dot(pt[...], rhs, preferred_element_type=jnp.float32)
    out[0] = r[:, :LANES].astype(out.dtype)
    out[1] = r[:, LANES:].astype(out.dtype)


def spread_back(pt, coupled):
    depth = pt.shape[0]
    blocks = coupled.shape[1]
    return pl.pallas_call(
        spread_kernel,
        grid=(blocks,),
        out_shape=jax.ShapeDtypeStruct((2, depth, blocks * LANES), jnp.bfloat16),
        in_specs=[
            pl.BlockSpec((depth, 2 * NP), lambda b: (0, 0)),
            pl.BlockSpec((2, 1, NP, LANES), lambda b: (0, b, 0, 0)),
        ],
        out_specs=pl.BlockSpec((2, depth, LANES), lambda b: (0, 0, b)),
        compiler_params=pltpu.CompilerParams(vmem_limit_bytes=32 * 2**20),
        name="spread_back",
    )(pt, coupled)


def solution(mesh):
    n_pw, n_band = mesh.shape["pw"], mesh.shape["band"]

    def shards(waves, projectors, coupling, offsets, counts):
        block = coupling_block(coupling, offsets, counts)
        pt, coupled = gather_coupled(n_pw, n_band, waves, projectors, block)
        return spread_back(pt, coupled)

    placed = (P(None, "pw", "band"), P(None, "band", "pw"), P(), P(), P())
    return jax.shard_map(
        shards, mesh=mesh, in_specs=placed, out_specs=P(None, "pw", "band"), check_vma=False
    )
```

```python
import functools

import jax
import jax.numpy as jnp
from jax import lax
from jax.experimental import pallas as pl
from jax.experimental.pallas import tpu as pltpu
from jax.sharding import PartitionSpec as P

NP = 128
M = 13
LANES = 128
SLOT = 16
MESH = pl.DeviceIdType.MESH


def coupling_block(coupling, offsets, counts, spare):
    atoms, most, _ = coupling.shape
    wide = spare.shape[0]
    spare[...] = jnp.zeros_like(spare)
    for a in range(atoms):
        spare[a * SLOT:a * SLOT + most, :most] = coupling[a]

    def iota(shape, dim):
        return lax.broadcasted_iota(jnp.int32, shape, dim)

    place = iota((NP, wide), 1)
    atom, entry = lax.div(place, SLOT), lax.rem(place, SLOT)
    start = jnp.full((NP, wide), -wide, jnp.int32)
    count = jnp.zeros((NP, wide), jnp.int32)
    for a in range(atoms):
        start = jnp.where(atom == a, offsets[a], start)
        count = jnp.where(atom == a, counts[a], count)
    select = jnp.where((iota((NP, wide), 0) == start + entry) & (entry < count), 1.0, 0.0)
    repeat = jnp.where(lax.rem(iota((LANES, wide), 1), SLOT) == iota((LANES, wide), 0), 1.0, 0.0)
    same = lax.div(iota((wide, wide), 0), SLOT) == lax.div(iota((wide, wide), 1), SLOT)
    spread = dot_exact(spare[...], repeat, 0)
    spread = jnp.where(same, spread, 0.0)
    raw = dot_exact(dot_exact(select, spread, 0), select, 1)
    return (raw + raw.T) * 0.5


def dot_exact(a, b, dim):
    return lax.dot_general(a, b, (((1,), (dim,)), ((), ())), precision=lax.Precision.HIGHEST,
                           preferred_element_type=jnp.float32)


def column_tiles(columns):
    return [(start, min(256, columns - start)) for start in range(0, columns, 256)]


def windows_of(n_band, pieces, held, piece):
    if n_band != 2 or held < 2 * SLOT:
        return [None] * (pieces - 1) + [(0, NP)]
    ends = [held + i * piece - SLOT for i in range(pieces - 1)] + [NP]
    return [(first, end - first) for first, end in zip([0] + ends[:-1], ends)]


def gather_kernel(n_pw, n_band, waves, proj, coupling, offsets, counts, pt_out, c_out,
                  w, p_all, acc, sib, send, recv, total, c_all, pt, spare, block,
                  w_sem, own_sem, out_sem, p_send, p_recv, s_send, s_recv,
                  r_send, r_recv, g_send, g_recv, f_send, f_recv):
    pw = lax.axis_index("pw")
    band = lax.axis_index("band")
    chip, core = lax.div(pw, 2), lax.rem(pw, 2)
    chips = n_pw // 2
    held = proj.shape[1]
    columns = waves.shape[2]
    blocks = columns // LANES
    piece = min(32, held)
    subs = held // piece
    tiles = column_tiles(columns)
    sibling = (chip * 2 + 1 - core, band)
    windows = windows_of(n_band, 1 + (n_band - 1) * subs, held, piece)

    def chip_at(step):
        return lax.rem(chip + step, chips)

    def same_core(other):
        return (other * 2 + core, band)

    def sub_of(sender, s):
        return subs - 1 - s + sender * (2 * s - subs + 1) if n_band == 2 else s

    def window(i):
        first, size = windows[i]
        if first == 0 and size == NP:
            return pl.ds(0, NP)
        return pl.ds(pl.multiple_of(first + band * (NP - 2 * first - size), SLOT), size)

    own_rows = pl.multiple_of(band * held, held)
    own = pltpu.make_async_copy(proj, p_all.at[:, pl.ds(own_rows, held), :], own_sem.at[0])
    own.start()
    wave_copies = []
    for t, (start, size) in enumerate(tiles):
        copy = pltpu.make_async_copy(
            waves.at[:, :, pl.ds(start, size)], w.at[:, :, pl.ds(start, size)], w_sem.at[t])
        copy.start()
        wave_copies.append(copy)

    barrier = pltpu.get_barrier_semaphore()
    for d in range(1, n_band):
        pl.semaphore_signal(barrier, inc=1, device_id=(pw, lax.rem(band + d, n_band)), device_id_type=MESH)
    pl.semaphore_signal(barrier, inc=1, device_id=sibling, device_id_type=MESH)
    for d in range(1, chips):
        pl.semaphore_signal(barrier, inc=1, device_id=same_core(chip_at(d)), device_id_type=MESH)
    pl.semaphore_wait(barrier, n_band - 1 + 1 + chips - 1)

    p_copies = []
    for d in range(1, n_band):
        for s in range(subs):
            sub = sub_of(band, s)
            rows = pl.ds(pl.multiple_of(band * held + sub * piece, piece), piece)
            copy = pltpu.make_async_remote_copy(
                src_ref=proj.at[:, pl.ds(pl.multiple_of(sub * piece, piece), piece), :],
                dst_ref=p_all.at[:, rows, :],
                send_sem=p_send.at[d - 1, s], recv_sem=p_recv.at[d - 1, s],
                device_id=(pw, lax.rem(band + d, n_band)), device_id_type=MESH)
            copy.start()
            p_copies.append(copy)

    pieces = [(own_rows, held)]
    for d in range(1, n_band):
        source = lax.rem(band + n_band - d, n_band)
        for s in range(subs):
            row = pl.multiple_of(source * held + sub_of(source, s) * piece, piece)
            pieces.append((row, piece))
    last = len(pieces) - 1

    def project(i):
        row, size = pieces[i]
        rows = pl.ds(row, size)
        p0, p1 = p_all[0, rows, :], p_all[1, rows, :]
        lhs0 = jnp.concatenate([p0, -p1], axis=0)
        lhs1 = jnp.concatenate([p1, p0], axis=0)
        for t, (start, width) in enumerate(tiles):
            if i == 0:
                wave_copies[t].wait()
            cols = pl.ds(start, width)
            r = jnp.dot(lhs0, w[0, :, cols], preferred_element_type=jnp.float32)
            r += jnp.dot(lhs1, w[1, :, cols], preferred_element_type=jnp.float32)
            acc[0, rows, cols] = r[:size]
            acc[1, rows, cols] = r[size:]

    def sibling_copy(i):
        rows = pl.ds(*pieces[i])
        return pltpu.make_async_remote_copy(
            src_ref=acc.at[1 - core, rows, :], dst_ref=sib.at[rows, :],
            send_sem=s_send.at[i], recv_sem=s_recv.at[i],
            device_id=sibling, device_id_type=MESH)

    def reduce_copy(i, d):
        other = chip_at(d)
        rows = pl.ds(*pieces[i])
        return pltpu.make_async_remote_copy(
            src_ref=send.at[lax.min(other, blocks - 1), rows, :],
            dst_ref=recv.at[chip, rows, :],
            send_sem=r_send.at[i, d], recv_sem=r_recv.at[i, chip],
            device_id=same_core(other), device_id_type=MESH)

    def reduce_send(i):
        rows = pl.ds(*pieces[i])
        sibling_copy(i).wait_recv()
        for b in range(blocks):
            cols = pl.ds(b * LANES, LANES)
            send[b, rows, :] = (acc[core, rows, cols] + sib[rows, cols]).astype(jnp.bfloat16)
        for d in range(1, chips):
            pl.when(chip_at(d) < blocks)(lambda: reduce_copy(i, d).start())

    def gather_copy(i, b, d):
        rows = window(i)
        return pltpu.make_async_remote_copy(
            src_ref=c_all.at[core, b, rows, :], dst_ref=c_all.at[core, b, rows, :],
            send_sem=g_send.at[i, d], recv_sem=g_recv.at[i, b],
            device_id=same_core(chip_at(d)), device_id_type=MESH)

    def forward_copy(i, k, b):
        rows = window(i)
        return pltpu.make_async_remote_copy(
            src_ref=c_all.at[k, b, rows, :], dst_ref=c_all.at[k, b, rows, :],
            send_sem=f_send.at[i, b], recv_sem=f_recv.at[i, b],
            device_id=sibling, device_id_type=MESH)

    def couple(i):
        rows = pl.ds(*pieces[i])

        @pl.when(chip < blocks)
        def _():
            value = send[chip, rows, :].astype(jnp.float32)
            for d in range(1, chips):
                source = chip_at(d)
                pltpu.make_async_remote_copy(
                    src_ref=send.at[0, rows, :], dst_ref=recv.at[source, rows, :],
                    send_sem=r_send.at[i, d], recv_sem=r_recv.at[i, source],
                    device_id=same_core(source), device_id_type=MESH).wait_recv()
                value += recv[source, rows, :].astype(jnp.float32)
            total[rows, :] = value
            if windows[i] is not None:
                c_all[core, chip, window(i), :] = dot_exact(
                    block[window(i), :], total[...], 0).astype(jnp.bfloat16)
                for d in range(1, chips):
                    gather_copy(i, chip, d).start()
                forward_copy(i, core, chip).start()

    def forward(i):
        if windows[i] is None:
            return
        for d in range(1, chips):
            source = chip_at(d)

            @pl.when(source < blocks)
            def _():
                gather_copy(i, source, d).wait_recv()
                forward_copy(i, core, source).start()

    total[...] = jnp.zeros_like(total)
    own.wait()
    project(0)
    sibling_copy(0).start()
    block[...] = coupling_block(coupling, offsets, counts, spare)
    reduce_send(0)
    for i in range(1, last + 1):
        p_copies[i - 1].wait_recv()
        project(i)
        sibling_copy(i).start()
        couple(i - 1)
        reduce_send(i)
        if i >= 2:
            forward(i - 2)

    pt[:, :NP] = p_all[0].T
    pt[:, NP:] = p_all[1].T
    pt_copy = pltpu.make_async_copy(pt, pt_out, out_sem.at[0])
    pt_copy.start()
    couple(last)
    if last >= 1:
        forward(last - 1)
    forward(last)

    wanted = [i for i in range(last + 1) if windows[i] is not None]
    for i in wanted:
        for b in range(blocks):
            forward_copy(i, 1 - core, b).wait_recv()
    c_copy = pltpu.make_async_copy(c_all, c_out, out_sem.at[1])
    c_copy.start()

    for copy in p_copies:
        copy.wait_send()
    for i in range(last + 1):
        sibling_copy(i).wait_send()
        for d in range(1, chips):
            pl.when(chip_at(d) < blocks)(lambda: reduce_copy(i, d).wait_send())

    @pl.when(chip < blocks)
    def _():
        for i in wanted:
            for d in range(1, chips):
                gather_copy(i, chip, d).wait_send()
    for i in wanted:
        for b in range(blocks):
            forward_copy(i, core, b).wait_send()
    pt_copy.wait()
    c_copy.wait()


def gather_coupled(n_pw, n_band, waves, projectors, coupling, offsets, counts):
    _, depth, columns = waves.shape
    held = projectors.shape[1]
    chips = n_pw // 2
    blocks = columns // LANES
    subs = held // min(32, held)
    pieces = 1 + (n_band - 1) * subs
    bf16, f32 = jnp.bfloat16, jnp.float32
    dma = pltpu.SemaphoreType.DMA
    hbm = pl.BlockSpec(memory_space=pltpu.HBM)
    anywhere = pl.BlockSpec(memory_space=pl.ANY)
    scalars = pl.BlockSpec(memory_space=pltpu.SMEM)
    wide = -(-coupling.shape[0] * SLOT // LANES) * LANES
    return pl.pallas_call(
        functools.partial(gather_kernel, n_pw, n_band),
        out_shape=[
            jax.ShapeDtypeStruct((depth, 2 * NP), bf16),
            jax.ShapeDtypeStruct((2, blocks, NP, LANES), bf16),
        ],
        in_specs=[hbm, hbm, pl.BlockSpec(memory_space=pltpu.VMEM), scalars, scalars],
        out_specs=[anywhere, anywhere],
        scratch_shapes=[
            pltpu.VMEM((2, depth, columns), bf16),
            pltpu.VMEM((2, NP, depth), bf16),
            pltpu.VMEM((2, NP, columns), f32),
            pltpu.VMEM((NP, columns), f32),
            pltpu.VMEM((blocks, NP, LANES), bf16),
            pltpu.VMEM((chips, NP, LANES), bf16),
            pltpu.VMEM((NP, LANES), f32),
            pltpu.VMEM((2, blocks, NP, LANES), bf16),
            pltpu.VMEM((depth, 2 * NP), bf16),
            pltpu.VMEM((wide, LANES), f32),
            pltpu.VMEM((NP, NP), f32),
            dma((len(column_tiles(columns)),)), dma((1,)), dma((2,)),
            dma((n_band - 1, subs)), dma((n_band - 1, subs)),
            dma((pieces,)), dma((pieces,)),
            dma((pieces, chips)), dma((pieces, chips)),
            dma((pieces, chips)), dma((pieces, blocks)),
            dma((pieces, blocks)), dma((pieces, blocks)),
        ],
        compiler_params=pltpu.CompilerParams(
            collective_id=0, has_side_effects=True, vmem_limit_bytes=60 * 2**20),
        name="gather_coupled",
    )(waves, projectors, coupling, offsets, counts)


def spread_kernel(pt, c, out, rhs):
    blocks = c.shape[1]

    @pl.when(pl.program_id(0) == 0)
    def _():
        for b in range(blocks):
            c0, c1 = c[0, b], c[1, b]
            rhs[b, :NP, :LANES] = c0
            rhs[b, :NP, LANES:] = c1
            rhs[b, NP:, :LANES] = -c1
            rhs[b, NP:, LANES:] = c0

    for b in range(blocks):
        r = jnp.dot(pt[...], rhs[b], preferred_element_type=jnp.float32)
        out[0, :, b * LANES:(b + 1) * LANES] = r[:, :LANES].astype(out.dtype)
        out[1, :, b * LANES:(b + 1) * LANES] = r[:, LANES:].astype(out.dtype)


def spread_back(pt, coupled):
    depth = pt.shape[0]
    blocks = coupled.shape[1]
    rows = 256 if depth % 256 == 0 else depth
    return pl.pallas_call(
        spread_kernel,
        grid=(depth // rows,),
        out_shape=jax.ShapeDtypeStruct((2, depth, blocks * LANES), jnp.bfloat16),
        in_specs=[
            pl.BlockSpec((rows, 2 * NP), lambda r: (r, 0)),
            pl.BlockSpec((2, blocks, NP, LANES), lambda r: (0, 0, 0, 0)),
        ],
        out_specs=pl.BlockSpec((2, rows, blocks * LANES), lambda r: (0, r, 0)),
        scratch_shapes=[pltpu.VMEM((blocks, 2 * NP, 2 * LANES), jnp.bfloat16)],
        compiler_params=pltpu.CompilerParams(vmem_limit_bytes=60 * 2**20),
        name="spread_back",
    )(pt, coupled)


def solution(mesh):
    n_pw, n_band = mesh.shape["pw"], mesh.shape["band"]

    def shards(waves, projectors, coupling, offsets, counts):
        pt, coupled = gather_coupled(n_pw, n_band, waves, projectors, coupling, offsets, counts)
        return spread_back(pt, coupled)

    placed = (P(None, "pw", "band"), P(None, "band", "pw"), P(), P(), P())
    return jax.shard_map(
        shards, mesh=mesh, in_specs=placed, out_specs=P(None, "pw", "band"), check_vma=False
    )
```

```python
import functools

import jax
import jax.numpy as jnp
from jax import lax
from jax.experimental import pallas as pl
from jax.experimental.pallas import tpu as pltpu
from jax.sharding import PartitionSpec as P

NP = 128
M = 13
LANES = 128
SLOT = 16
MESH = pl.DeviceIdType.MESH


def coupling_block(coupling, offsets, counts, spare):
    atoms, most, _ = coupling.shape
    wide = spare.shape[0]
    spare[...] = jnp.zeros_like(spare)
    for a in range(atoms):
        spare[a * SLOT:a * SLOT + most, :most] = coupling[a]

    def iota(shape, dim):
        return lax.broadcasted_iota(jnp.int32, shape, dim)

    place = iota((NP, wide), 1)
    atom, entry = lax.div(place, SLOT), lax.rem(place, SLOT)
    start = jnp.full((NP, wide), -wide, jnp.int32)
    count = jnp.zeros((NP, wide), jnp.int32)
    for a in range(atoms):
        start = jnp.where(atom == a, offsets[a], start)
        count = jnp.where(atom == a, counts[a], count)
    select = jnp.where((iota((NP, wide), 0) == start + entry) & (entry < count), 1.0, 0.0)
    repeat = jnp.where(lax.rem(iota((LANES, wide), 1), SLOT) == iota((LANES, wide), 0), 1.0, 0.0)
    same = lax.div(iota((wide, wide), 0), SLOT) == lax.div(iota((wide, wide), 1), SLOT)
    spread = dot_exact(spare[...], repeat, 0)
    spread = jnp.where(same, spread, 0.0)
    raw = dot_exact(dot_exact(select, spread, 0), select, 1)
    return (raw + raw.T) * 0.5


def dot_exact(a, b, dim):
    return lax.dot_general(a, b, (((1,), (dim,)), ((), ())), precision=lax.Precision.HIGHEST,
                           preferred_element_type=jnp.float32)


def column_tiles(columns):
    return [(start, min(256, columns - start)) for start in range(0, columns, 256)]


def pieces_of(n_band, held):
    return [held - SLOT, SLOT] if n_band == 2 and held > SLOT else [held]


def windows_of(n_band, held):
    sizes = pieces_of(n_band, held)
    if n_band != 2 or held <= SLOT:
        return [None] * ((n_band - 1) * len(sizes)) + [(0, NP)]
    ends = [held - SLOT] + [held + sum(sizes[:s + 1]) - SLOT for s in range(len(sizes))]
    ends[-1] = NP
    return [(first, end - first) for first, end in zip([0] + ends[:-1], ends)]


def gather_kernel(n_pw, n_band, waves, proj, coupling, offsets, counts, pt_out, c_out,
                  w, p_all, acc, sib, send, recv, last_send, last_recv, total, c_all, pt, spare, block,
                  w_sem, own_sem, out_sem, p_send, p_recv, s_send, s_recv,
                  r_send, r_recv, l_send, l_recv, g_send, g_recv, f_send, f_recv, h_send, h_recv):
    pw = lax.axis_index("pw")
    band = lax.axis_index("band")
    chip, core = lax.div(pw, 2), lax.rem(pw, 2)
    chips = n_pw // 2
    held = proj.shape[1]
    columns = waves.shape[2]
    blocks = columns // LANES
    sizes = pieces_of(n_band, held)
    tiles = column_tiles(columns)
    sibling = (chip * 2 + 1 - core, band)
    windows = windows_of(n_band, held)
    bf16 = jnp.bfloat16

    def chip_at(step):
        return lax.rem(chip + step, chips)

    def pw_at(step):
        return lax.rem(pw + step, n_pw)

    def same_core(other):
        return (other * 2 + core, band)

    def sub_row(sender, s):
        if n_band != 2:
            return 0
        first = sum(sizes[:s])
        return pl.multiple_of(first + (1 - sender) * (held - 2 * first - sizes[s]), SLOT)

    def window(i):
        first, size = windows[i]
        if first == 0 and size == NP:
            return pl.ds(0, NP)
        return pl.ds(pl.multiple_of(first + band * (NP - 2 * first - size), SLOT), size)

    own_rows = pl.multiple_of(band * held, held)
    own = pltpu.make_async_copy(proj, p_all.at[:, pl.ds(own_rows, held), :], own_sem.at[0])
    own.start()
    wave_copies = []
    for t, (start, size) in enumerate(tiles):
        copy = pltpu.make_async_copy(
            waves.at[:, :, pl.ds(start, size)], w.at[:, :, pl.ds(start, size)], w_sem.at[t])
        copy.start()
        wave_copies.append(copy)

    barrier = pltpu.get_barrier_semaphore()
    for d in range(1, n_pw):
        pl.semaphore_signal(barrier, inc=1, device_id=(pw_at(d), band), device_id_type=MESH)
    for d in range(1, n_band):
        pl.semaphore_signal(barrier, inc=1, device_id=(pw, lax.rem(band + d, n_band)), device_id_type=MESH)
    pl.semaphore_wait(barrier, n_band - 1 + n_pw - 1)

    p_copies = []
    for d in range(1, n_band):
        for s, size in enumerate(sizes):
            row = sub_row(band, s)
            copy = pltpu.make_async_remote_copy(
                src_ref=proj.at[:, pl.ds(row, size), :],
                dst_ref=p_all.at[:, pl.ds(pl.multiple_of(own_rows + row, SLOT), size), :],
                send_sem=p_send.at[d - 1, s], recv_sem=p_recv.at[d - 1, s],
                device_id=(pw, lax.rem(band + d, n_band)), device_id_type=MESH)
            copy.start()
            p_copies.append(copy)

    pieces = [(own_rows, held)]
    for d in range(1, n_band):
        source = lax.rem(band + n_band - d, n_band)
        for s, size in enumerate(sizes):
            pieces.append((pl.multiple_of(source * held + sub_row(source, s), SLOT), size))
    last = len(pieces) - 1

    def project(i):
        row, size = pieces[i]
        rows = pl.ds(row, size)
        p0, p1 = p_all[0, rows, :], p_all[1, rows, :]
        lhs0 = jnp.concatenate([p0, -p1], axis=0)
        lhs1 = jnp.concatenate([p1, p0], axis=0)
        for t, (start, width) in enumerate(tiles):
            if i == 0:
                wave_copies[t].wait()
            cols = pl.ds(start, width)
            r = jnp.dot(lhs0, w[0, :, cols], preferred_element_type=jnp.float32)
            r += jnp.dot(lhs1, w[1, :, cols], preferred_element_type=jnp.float32)
            if i == last:
                for c in range(0, width, LANES):
                    last_send[0, (start + c) // LANES] = r[:size, c:c + LANES].astype(bf16)
                    last_send[1, (start + c) // LANES] = r[size:, c:c + LANES].astype(bf16)
            else:
                acc[0, rows, cols] = r[:size]
                acc[1, rows, cols] = r[size:]

    def sibling_copy(i):
        rows = pl.ds(*pieces[i])
        return pltpu.make_async_remote_copy(
            src_ref=acc.at[1 - core, rows, :], dst_ref=sib.at[rows, :],
            send_sem=s_send.at[i], recv_sem=s_recv.at[i],
            device_id=sibling, device_id_type=MESH)

    def reduce_copy(i, d):
        other = chip_at(d)
        rows = pl.ds(*pieces[i])
        return pltpu.make_async_remote_copy(
            src_ref=send.at[lax.min(other, blocks - 1), rows, :],
            dst_ref=recv.at[chip, rows, :],
            send_sem=r_send.at[i, d], recv_sem=r_recv.at[i, chip],
            device_id=same_core(other), device_id_type=MESH)

    def reduce_send(i):
        rows = pl.ds(*pieces[i])
        sibling_copy(i).wait_recv()
        for b in range(blocks):
            cols = pl.ds(b * LANES, LANES)
            send[b, rows, :] = (acc[core, rows, cols] + sib[rows, cols]).astype(bf16)
        for d in range(1, chips):
            pl.when(chip_at(d) < blocks)(lambda: reduce_copy(i, d).start())

    def last_copy(e):
        target = pw_at(e)
        return pltpu.make_async_remote_copy(
            src_ref=last_send.at[lax.rem(target, 2), lax.min(lax.div(target, 2), blocks - 1)],
            dst_ref=last_recv.at[pw],
            send_sem=l_send.at[e], recv_sem=l_recv.at[pw],
            device_id=(target, band), device_id_type=MESH)

    def gather_copy(i, b, d):
        rows = window(i)
        return pltpu.make_async_remote_copy(
            src_ref=c_all.at[core, b, rows, :], dst_ref=c_all.at[core, b, rows, :],
            send_sem=g_send.at[i, d], recv_sem=g_recv.at[i, b],
            device_id=same_core(chip_at(d)), device_id_type=MESH)

    def forward_copy(i, k, b):
        rows = window(i)
        return pltpu.make_async_remote_copy(
            src_ref=c_all.at[k, b, rows, :], dst_ref=c_all.at[k, b, rows, :],
            send_sem=f_send.at[i, b], recv_sem=f_recv.at[i, b],
            device_id=sibling, device_id_type=MESH)

    def final_copy(owner, e):
        here = c_all.at[lax.rem(owner, 2), lax.min(lax.div(owner, 2), blocks - 1), window(last), :]
        return pltpu.make_async_remote_copy(
            src_ref=here, dst_ref=here, send_sem=h_send.at[e], recv_sem=h_recv.at[owner],
            device_id=(pw_at(e), band), device_id_type=MESH)

    def couple(i):
        rows = pl.ds(*pieces[i])
        if i == last:
            value = last_send[core, chip].astype(jnp.float32)
            for e in range(1, n_pw):
                source = pw_at(e)
                pltpu.make_async_remote_copy(
                    src_ref=last_send.at[0, 0], dst_ref=last_recv.at[source],
                    send_sem=l_send.at[e], recv_sem=l_recv.at[source],
                    device_id=(source, band), device_id_type=MESH).wait_recv()
                value += last_recv[source].astype(jnp.float32)
        else:
            value = send[chip, rows, :].astype(jnp.float32)
            for d in range(1, chips):
                source = chip_at(d)
                pltpu.make_async_remote_copy(
                    src_ref=send.at[0, rows, :], dst_ref=recv.at[source, rows, :],
                    send_sem=r_send.at[i, d], recv_sem=r_recv.at[i, source],
                    device_id=same_core(source), device_id_type=MESH).wait_recv()
                value += recv[source, rows, :].astype(jnp.float32)
        total[rows, :] = value
        if windows[i] is None:
            return
        c_all[core, chip, window(i), :] = dot_exact(block[window(i), :], total[...], 0).astype(bf16)
        if i == last:
            for e in range(1, n_pw):
                final_copy(pw, e).start()
        else:
            for d in range(1, chips):
                gather_copy(i, chip, d).start()
            forward_copy(i, core, chip).start()

    def forward(i):
        for d in range(1, chips):
            source = chip_at(d)

            @pl.when(source < blocks)
            def _():
                gather_copy(i, source, d).wait_recv()
                forward_copy(i, core, source).start()

    def out_copy(i):
        rows = window(i)
        return pltpu.make_async_copy(
            c_all.at[:, :, rows, :], c_out.at[:, :, rows, :], out_sem.at[i + 1])

    early = [i for i in range(last) if windows[i] is not None]
    owns = chip < blocks

    own.wait()
    project(0)
    if last > 0:
        sibling_copy(0).start()
        total[...] = jnp.zeros_like(total)
        reduce_send(0)
    block[...] = coupling_block(coupling, offsets, counts, spare)
    for i in range(1, last + 1):
        p_copies[i - 1].wait_recv()
        project(i)
        if i < last:
            sibling_copy(i).start()
            reduce_send(i)
    for e in range(1, n_pw):
        pl.when(lax.div(pw_at(e), 2) < blocks)(lambda: last_copy(e).start())

    for i in range(last):
        pl.when(owns)(lambda: couple(i))

    pt[:, :NP] = p_all[0].T
    pt[:, NP:] = p_all[1].T
    pt_copy = pltpu.make_async_copy(pt, pt_out, out_sem.at[0])
    pt_copy.start()
    for copy in p_copies:
        copy.wait_send()
    for i in range(last):
        sibling_copy(i).wait_send()
        for d in range(1, chips):
            pl.when(chip_at(d) < blocks)(lambda: reduce_copy(i, d).wait_send())

    pl.when(owns)(lambda: couple(last))
    for i in early:
        forward(i)
    for i in early:
        for b in range(blocks):
            forward_copy(i, 1 - core, b).wait_recv()
        out_copy(i).start()
    for e in range(1, n_pw):
        pl.when(lax.div(pw_at(e), 2) < blocks)(lambda: final_copy(pw_at(e), e).wait_recv())
    out_copy(last).start()

    for e in range(1, n_pw):
        pl.when(lax.div(pw_at(e), 2) < blocks)(lambda: last_copy(e).wait_send())

    @pl.when(owns)
    def _():
        for i in early:
            for d in range(1, chips):
                gather_copy(i, chip, d).wait_send()
        for e in range(1, n_pw):
            final_copy(pw, e).wait_send()
    for i in early:
        for b in range(blocks):
            forward_copy(i, core, b).wait_send()
        out_copy(i).wait()
    pt_copy.wait()
    out_copy(last).wait()


def gather_coupled(n_pw, n_band, waves, projectors, coupling, offsets, counts):
    _, depth, columns = waves.shape
    held = projectors.shape[1]
    chips = n_pw // 2
    blocks = columns // LANES
    sizes = pieces_of(n_band, held)
    subs = len(sizes)
    pieces = 1 + (n_band - 1) * subs
    last_rows = sizes[-1]
    bf16, f32 = jnp.bfloat16, jnp.float32
    dma = pltpu.SemaphoreType.DMA
    hbm = pl.BlockSpec(memory_space=pltpu.HBM)
    anywhere = pl.BlockSpec(memory_space=pl.ANY)
    scalars = pl.BlockSpec(memory_space=pltpu.SMEM)
    wide = -(-coupling.shape[0] * SLOT // LANES) * LANES
    return pl.pallas_call(
        functools.partial(gather_kernel, n_pw, n_band),
        out_shape=[
            jax.ShapeDtypeStruct((depth, 2 * NP), bf16),
            jax.ShapeDtypeStruct((2, blocks, NP, LANES), bf16),
        ],
        in_specs=[hbm, hbm, pl.BlockSpec(memory_space=pltpu.VMEM), scalars, scalars],
        out_specs=[anywhere, anywhere],
        scratch_shapes=[
            pltpu.VMEM((2, depth, columns), bf16),
            pltpu.VMEM((2, NP, depth), bf16),
            pltpu.VMEM((2, NP, columns), f32),
            pltpu.VMEM((NP, columns), f32),
            pltpu.VMEM((blocks, NP, LANES), bf16),
            pltpu.VMEM((chips, NP, LANES), bf16),
            pltpu.VMEM((2, blocks, last_rows, LANES), bf16),
            pltpu.VMEM((n_pw, last_rows, LANES), bf16),
            pltpu.VMEM((NP, LANES), f32),
            pltpu.VMEM((2, blocks, NP, LANES), bf16),
            pltpu.VMEM((depth, 2 * NP), bf16),
            pltpu.VMEM((wide, LANES), f32),
            pltpu.VMEM((NP, NP), f32),
            dma((len(column_tiles(columns)),)), dma((1,)), dma((1 + pieces,)),
            dma((n_band - 1, subs)), dma((n_band - 1, subs)),
            dma((pieces,)), dma((pieces,)),
            dma((pieces, chips)), dma((pieces, chips)),
            dma((n_pw,)), dma((n_pw,)),
            dma((pieces, chips)), dma((pieces, blocks)),
            dma((pieces, blocks)), dma((pieces, blocks)),
            dma((n_pw,)), dma((n_pw,)),
        ],
        compiler_params=pltpu.CompilerParams(
            collective_id=0, has_side_effects=True, vmem_limit_bytes=60 * 2**20),
        name="gather_coupled",
    )(waves, projectors, coupling, offsets, counts)


def row_parts(depth):
    ends = list(range(512, depth, 512)) + [depth]
    return [(first, end - first) for first, end in zip([0] + ends[:-1], ends)]


def spread_kernel(pt, c, out, pt_vmem, c_vmem, rhs, result, in_sem, out_sem):
    blocks = c.shape[1]
    parts = row_parts(pt.shape[0])
    c_copy = pltpu.make_async_copy(c, c_vmem, in_sem.at[0])
    c_copy.start()
    pt_copies = []
    for i, (first, size) in enumerate(parts):
        rows = pl.ds(first, size)
        copy = pltpu.make_async_copy(pt.at[rows, :], pt_vmem.at[rows, :], in_sem.at[i + 1])
        copy.start()
        pt_copies.append(copy)
    c_copy.wait()
    for b in range(blocks):
        c0, c1 = c_vmem[0, b], c_vmem[1, b]
        rhs[b, :NP, :LANES] = c0
        rhs[b, :NP, LANES:] = c1
        rhs[b, NP:, :LANES] = -c1
        rhs[b, NP:, LANES:] = c0
    out_copies = []
    for i, (first, size) in enumerate(parts):
        rows = pl.ds(first, size)
        pt_copies[i].wait()
        for b in range(blocks):
            cols = pl.ds(b * LANES, LANES)
            r = jnp.dot(pt_vmem[rows, :], rhs[b], preferred_element_type=jnp.float32)
            result[0, rows, cols] = r[:, :LANES].astype(result.dtype)
            result[1, rows, cols] = r[:, LANES:].astype(result.dtype)
        for k in range(2):
            copy = pltpu.make_async_copy(
                result.at[k, rows, :], out.at[k, rows, :], out_sem.at[i, k])
            copy.start()
            out_copies.append(copy)
    for copy in out_copies:
        copy.wait()


def spread_back(pt, coupled):
    depth = pt.shape[0]
    blocks = coupled.shape[1]
    parts = len(row_parts(depth))
    bf16 = jnp.bfloat16
    anywhere = pl.BlockSpec(memory_space=pl.ANY)
    return pl.pallas_call(
        spread_kernel,
        out_shape=jax.ShapeDtypeStruct((2, depth, blocks * LANES), bf16),
        in_specs=[anywhere, anywhere],
        out_specs=anywhere,
        scratch_shapes=[
            pltpu.VMEM(pt.shape, bf16),
            pltpu.VMEM(coupled.shape, bf16),
            pltpu.VMEM((blocks, 2 * NP, 2 * LANES), bf16),
            pltpu.VMEM((2, depth, blocks * LANES), bf16),
            pltpu.SemaphoreType.DMA((1 + parts,)),
            pltpu.SemaphoreType.DMA((parts, 2)),
        ],
        compiler_params=pltpu.CompilerParams(vmem_limit_bytes=60 * 2**20),
        name="spread_back",
    )(pt, coupled)


def solution(mesh):
    n_pw, n_band = mesh.shape["pw"], mesh.shape["band"]

    def shards(waves, projectors, coupling, offsets, counts):
        pt, coupled = gather_coupled(n_pw, n_band, waves, projectors, coupling, offsets, counts)
        return spread_back(pt, coupled)

    placed = (P(None, "pw", "band"), P(None, "band", "pw"), P(), P(), P())
    return jax.shard_map(
        shards, mesh=mesh, in_specs=placed, out_specs=P(None, "pw", "band"), check_vma=False
    )
```

```python
import functools

import jax
import jax.numpy as jnp
from jax import lax
from jax.experimental import pallas as pl
from jax.experimental.pallas import tpu as pltpu
from jax.sharding import PartitionSpec as P

NP = 128
M = 13
LANES = 128
SLOT = 16
MESH = pl.DeviceIdType.MESH


def coupling_block(coupling, offsets, counts, spare):
    atoms, most, _ = coupling.shape
    wide = spare.shape[0]
    spare[...] = jnp.zeros_like(spare)
    for a in range(atoms):
        spare[a * SLOT:a * SLOT + most, :most] = coupling[a]

    def iota(shape, dim):
        return lax.broadcasted_iota(jnp.int32, shape, dim)

    place = iota((NP, wide), 1)
    atom, entry = lax.div(place, SLOT), lax.rem(place, SLOT)
    start = jnp.full((NP, wide), -wide, jnp.int32)
    count = jnp.zeros((NP, wide), jnp.int32)
    for a in range(atoms):
        start = jnp.where(atom == a, offsets[a], start)
        count = jnp.where(atom == a, counts[a], count)
    select = jnp.where((iota((NP, wide), 0) == start + entry) & (entry < count), 1.0, 0.0)
    repeat = jnp.where(lax.rem(iota((LANES, wide), 1), SLOT) == iota((LANES, wide), 0), 1.0, 0.0)
    same = lax.div(iota((wide, wide), 0), SLOT) == lax.div(iota((wide, wide), 1), SLOT)
    spread = dot_exact(spare[...], repeat, 0)
    spread = jnp.where(same, spread, 0.0)
    raw = dot_exact(dot_exact(select, spread, 0), select, 1)
    return (raw + raw.T) * 0.5


def dot_exact(a, b, dim):
    return lax.dot_general(a, b, (((1,), (dim,)), ((), ())), precision=lax.Precision.HIGHEST,
                           preferred_element_type=jnp.float32)


def column_tiles(columns):
    return [(start, min(256, columns - start)) for start in range(0, columns, 256)]


def pieces_of(n_band, held):
    return [held - SLOT, SLOT] if n_band == 2 and held > SLOT else [held]


def windows_of(n_band, held):
    sizes = pieces_of(n_band, held)
    if n_band != 2 or held <= SLOT:
        return [None] * ((n_band - 1) * len(sizes)) + [(0, NP)]
    early = NP - sizes[-1] - SLOT
    return [None] * (len(sizes) - 1) + [(0, early), (early, NP - early)]


def gather_kernel(n_pw, n_band, waves, proj, coupling, offsets, counts, pt_out, c_out,
                  w, p_all, acc, sib, send, recv, last_send, last_recv, total, c_all, pt, spare, block,
                  w_sem, own_sem, out_sem, p_send, p_recv, s_send, s_recv,
                  r_send, r_recv, l_send, l_recv, g_send, g_recv, f_send, f_recv, h_send, h_recv):
    pw = lax.axis_index("pw")
    band = lax.axis_index("band")
    chip, core = lax.div(pw, 2), lax.rem(pw, 2)
    chips = n_pw // 2
    held = proj.shape[1]
    columns = waves.shape[2]
    blocks = columns // LANES
    sizes = pieces_of(n_band, held)
    tiles = column_tiles(columns)
    sibling = (chip * 2 + 1 - core, band)
    windows = windows_of(n_band, held)
    bf16 = jnp.bfloat16

    def chip_at(step):
        return lax.rem(chip + step, chips)

    def pw_at(step):
        return lax.rem(pw + step, n_pw)

    def same_core(other):
        return (other * 2 + core, band)

    def sub_row(sender, s):
        if n_band != 2:
            return 0
        first = sum(sizes[:s])
        return pl.multiple_of(first + (1 - sender) * (held - 2 * first - sizes[s]), SLOT)

    def window(i):
        first, size = windows[i]
        if first == 0 and size == NP:
            return pl.ds(0, NP)
        return pl.ds(pl.multiple_of(first + band * (NP - 2 * first - size), SLOT), size)

    own_rows = pl.multiple_of(band * held, held)
    own = pltpu.make_async_copy(proj, p_all.at[:, pl.ds(own_rows, held), :], own_sem.at[0])
    own.start()
    wave_copies = []
    for t, (start, size) in enumerate(tiles):
        copy = pltpu.make_async_copy(
            waves.at[:, :, pl.ds(start, size)], w.at[:, :, pl.ds(start, size)], w_sem.at[t])
        copy.start()
        wave_copies.append(copy)

    barrier = pltpu.get_barrier_semaphore()
    for d in range(1, n_pw):
        pl.semaphore_signal(barrier, inc=1, device_id=(pw_at(d), band), device_id_type=MESH)
    for d in range(1, n_band):
        pl.semaphore_signal(barrier, inc=1, device_id=(pw, lax.rem(band + d, n_band)), device_id_type=MESH)
    pl.semaphore_wait(barrier, n_band - 1 + n_pw - 1)

    p_copies = []
    for d in range(1, n_band):
        for s, size in enumerate(sizes):
            row = sub_row(band, s)
            copy = pltpu.make_async_remote_copy(
                src_ref=proj.at[:, pl.ds(row, size), :],
                dst_ref=p_all.at[:, pl.ds(pl.multiple_of(own_rows + row, SLOT), size), :],
                send_sem=p_send.at[d - 1, s], recv_sem=p_recv.at[d - 1, s],
                device_id=(pw, lax.rem(band + d, n_band)), device_id_type=MESH)
            copy.start()
            p_copies.append(copy)

    pieces = [(own_rows, held)]
    for d in range(1, n_band):
        source = lax.rem(band + n_band - d, n_band)
        for s, size in enumerate(sizes):
            pieces.append((pl.multiple_of(source * held + sub_row(source, s), SLOT), size))
    last = len(pieces) - 1

    def project(i):
        row, size = pieces[i]
        rows = pl.ds(row, size)
        p0, p1 = p_all[0, rows, :], p_all[1, rows, :]
        lhs0 = jnp.concatenate([p0, -p1], axis=0)
        lhs1 = jnp.concatenate([p1, p0], axis=0)
        for t, (start, width) in enumerate(tiles):
            if i == 0:
                wave_copies[t].wait()
            cols = pl.ds(start, width)
            r = jnp.dot(lhs0, w[0, :, cols], preferred_element_type=jnp.float32)
            r += jnp.dot(lhs1, w[1, :, cols], preferred_element_type=jnp.float32)
            if i == last:
                for c in range(0, width, LANES):
                    last_send[0, (start + c) // LANES] = r[:size, c:c + LANES].astype(bf16)
                    last_send[1, (start + c) // LANES] = r[size:, c:c + LANES].astype(bf16)
            else:
                acc[0, rows, cols] = r[:size]
                acc[1, rows, cols] = r[size:]

    def sibling_copy(i):
        rows = pl.ds(*pieces[i])
        return pltpu.make_async_remote_copy(
            src_ref=acc.at[1 - core, rows, :], dst_ref=sib.at[rows, :],
            send_sem=s_send.at[i], recv_sem=s_recv.at[i],
            device_id=sibling, device_id_type=MESH)

    def reduce_copy(i, d):
        other = chip_at(d)
        rows = pl.ds(*pieces[i])
        return pltpu.make_async_remote_copy(
            src_ref=send.at[lax.min(other, blocks - 1), rows, :],
            dst_ref=recv.at[chip, rows, :],
            send_sem=r_send.at[i, d], recv_sem=r_recv.at[i, chip],
            device_id=same_core(other), device_id_type=MESH)

    def reduce_send(i):
        rows = pl.ds(*pieces[i])
        sibling_copy(i).wait_recv()
        for b in range(blocks):
            cols = pl.ds(b * LANES, LANES)
            send[b, rows, :] = (acc[core, rows, cols] + sib[rows, cols]).astype(bf16)
        for d in range(1, chips):
            pl.when(chip_at(d) < blocks)(lambda: reduce_copy(i, d).start())

    def last_copy(e):
        target = pw_at(e)
        return pltpu.make_async_remote_copy(
            src_ref=last_send.at[lax.rem(target, 2), lax.min(lax.div(target, 2), blocks - 1)],
            dst_ref=last_recv.at[pw],
            send_sem=l_send.at[e], recv_sem=l_recv.at[pw],
            device_id=(target, band), device_id_type=MESH)

    def gather_copy(i, b, d):
        rows = window(i)
        return pltpu.make_async_remote_copy(
            src_ref=c_all.at[core, b, rows, :], dst_ref=c_all.at[core, b, rows, :],
            send_sem=g_send.at[i, d], recv_sem=g_recv.at[i, b],
            device_id=same_core(chip_at(d)), device_id_type=MESH)

    def forward_copy(i, k, b):
        rows = window(i)
        return pltpu.make_async_remote_copy(
            src_ref=c_all.at[k, b, rows, :], dst_ref=c_all.at[k, b, rows, :],
            send_sem=f_send.at[i, b], recv_sem=f_recv.at[i, b],
            device_id=sibling, device_id_type=MESH)

    def final_copy(owner, e):
        here = c_all.at[lax.rem(owner, 2), lax.min(lax.div(owner, 2), blocks - 1), window(last), :]
        return pltpu.make_async_remote_copy(
            src_ref=here, dst_ref=here, send_sem=h_send.at[e], recv_sem=h_recv.at[owner],
            device_id=(pw_at(e), band), device_id_type=MESH)

    def couple(i):
        rows = pl.ds(*pieces[i])
        if i == last:
            value = last_send[core, chip].astype(jnp.float32)
            for e in range(1, n_pw):
                source = pw_at(e)
                pltpu.make_async_remote_copy(
                    src_ref=last_send.at[0, 0], dst_ref=last_recv.at[source],
                    send_sem=l_send.at[e], recv_sem=l_recv.at[source],
                    device_id=(source, band), device_id_type=MESH).wait_recv()
                value += last_recv[source].astype(jnp.float32)
        else:
            value = send[chip, rows, :].astype(jnp.float32)
            for d in range(1, chips):
                source = chip_at(d)
                pltpu.make_async_remote_copy(
                    src_ref=send.at[0, rows, :], dst_ref=recv.at[source, rows, :],
                    send_sem=r_send.at[i, d], recv_sem=r_recv.at[i, source],
                    device_id=same_core(source), device_id_type=MESH).wait_recv()
                value += recv[source, rows, :].astype(jnp.float32)
        total[rows, :] = value
        if windows[i] is None:
            return
        c_all[core, chip, window(i), :] = dot_exact(block[window(i), :], total[...], 0).astype(bf16)
        if i == last:
            for e in range(1, n_pw):
                final_copy(pw, e).start()
        else:
            for d in range(1, chips):
                gather_copy(i, chip, d).start()
            forward_copy(i, core, chip).start()

    def forward(i):
        for d in range(1, chips):
            source = chip_at(d)

            @pl.when(source < blocks)
            def _():
                gather_copy(i, source, d).wait_recv()
                forward_copy(i, core, source).start()

    def out_copy(i):
        rows = window(i)
        return pltpu.make_async_copy(
            c_all.at[:, :, rows, :], c_out.at[:, :, rows, :], out_sem.at[i + 1])

    early = [i for i in range(last) if windows[i] is not None]
    owns = chip < blocks

    own.wait()
    project(0)
    if last > 0:
        sibling_copy(0).start()
        total[...] = jnp.zeros_like(total)
        reduce_send(0)
    block[...] = coupling_block(coupling, offsets, counts, spare)
    for i in range(1, last + 1):
        p_copies[i - 1].wait_recv()
        project(i)
        if i < last:
            sibling_copy(i).start()
            reduce_send(i)
    for e in range(1, n_pw):
        pl.when(lax.div(pw_at(e), 2) < blocks)(lambda: last_copy(e).start())

    for i in range(last + 1):
        pl.when(owns)(lambda: couple(i))
    for i in early:
        forward(i)

    pt[:, :NP] = p_all[0].T
    pt[:, NP:] = p_all[1].T
    pt_copy = pltpu.make_async_copy(pt, pt_out, out_sem.at[0])
    pt_copy.start()
    for i in early:
        for b in range(blocks):
            forward_copy(i, 1 - core, b).wait_recv()
        out_copy(i).start()

    for copy in p_copies:
        copy.wait_send()
    for i in range(last):
        sibling_copy(i).wait_send()
        for d in range(1, chips):
            pl.when(chip_at(d) < blocks)(lambda: reduce_copy(i, d).wait_send())
    for e in range(1, n_pw):
        pl.when(lax.div(pw_at(e), 2) < blocks)(lambda: last_copy(e).wait_send())

    @pl.when(owns)
    def _():
        for i in early:
            for d in range(1, chips):
                gather_copy(i, chip, d).wait_send()
        for e in range(1, n_pw):
            final_copy(pw, e).wait_send()
    for i in early:
        for b in range(blocks):
            forward_copy(i, core, b).wait_send()

    for e in range(1, n_pw):
        pl.when(lax.div(pw_at(e), 2) < blocks)(lambda: final_copy(pw_at(e), e).wait_recv())
    out_copy(last).start()
    pt_copy.wait()
    for i in early:
        out_copy(i).wait()
    out_copy(last).wait()


def gather_coupled(n_pw, n_band, waves, projectors, coupling, offsets, counts):
    _, depth, columns = waves.shape
    held = projectors.shape[1]
    chips = n_pw // 2
    blocks = columns // LANES
    sizes = pieces_of(n_band, held)
    subs = len(sizes)
    pieces = 1 + (n_band - 1) * subs
    last_rows = sizes[-1]
    bf16, f32 = jnp.bfloat16, jnp.float32
    dma = pltpu.SemaphoreType.DMA
    hbm = pl.BlockSpec(memory_space=pltpu.HBM)
    anywhere = pl.BlockSpec(memory_space=pl.ANY)
    scalars = pl.BlockSpec(memory_space=pltpu.SMEM)
    wide = -(-coupling.shape[0] * SLOT // LANES) * LANES
    return pl.pallas_call(
        functools.partial(gather_kernel, n_pw, n_band),
        out_shape=[
            jax.ShapeDtypeStruct((depth, 2 * NP), bf16),
            jax.ShapeDtypeStruct((2, blocks, NP, LANES), bf16),
        ],
        in_specs=[hbm, hbm, pl.BlockSpec(memory_space=pltpu.VMEM), scalars, scalars],
        out_specs=[anywhere, anywhere],
        scratch_shapes=[
            pltpu.VMEM((2, depth, columns), bf16),
            pltpu.VMEM((2, NP, depth), bf16),
            pltpu.VMEM((2, NP, columns), f32),
            pltpu.VMEM((NP, columns), f32),
            pltpu.VMEM((blocks, NP, LANES), bf16),
            pltpu.VMEM((chips, NP, LANES), bf16),
            pltpu.VMEM((2, blocks, last_rows, LANES), bf16),
            pltpu.VMEM((n_pw, last_rows, LANES), bf16),
            pltpu.VMEM((NP, LANES), f32),
            pltpu.VMEM((2, blocks, NP, LANES), bf16),
            pltpu.VMEM((depth, 2 * NP), bf16),
            pltpu.VMEM((wide, LANES), f32),
            pltpu.VMEM((NP, NP), f32),
            dma((len(column_tiles(columns)),)), dma((1,)), dma((1 + pieces,)),
            dma((n_band - 1, subs)), dma((n_band - 1, subs)),
            dma((pieces,)), dma((pieces,)),
            dma((pieces, chips)), dma((pieces, chips)),
            dma((n_pw,)), dma((n_pw,)),
            dma((pieces, chips)), dma((pieces, blocks)),
            dma((pieces, blocks)), dma((pieces, blocks)),
            dma((n_pw,)), dma((n_pw,)),
        ],
        compiler_params=pltpu.CompilerParams(
            collective_id=0, has_side_effects=True, vmem_limit_bytes=60 * 2**20),
        name="gather_coupled",
    )(waves, projectors, coupling, offsets, counts)


def row_parts(depth):
    ends = [end for end in (128, 512, 1024) if end < depth] + [depth]
    return [(first, end - first) for first, end in zip([0] + ends[:-1], ends)]


def spread_kernel(pt, c, out, pt_vmem, c_vmem, rhs, result, in_sem, out_sem):
    blocks = c.shape[1]
    parts = row_parts(pt.shape[0])
    c_copy = pltpu.make_async_copy(c, c_vmem, in_sem.at[0])
    c_copy.start()
    pt_copies = []
    for i, (first, size) in enumerate(parts):
        rows = pl.ds(first, size)
        copy = pltpu.make_async_copy(pt.at[rows, :], pt_vmem.at[rows, :], in_sem.at[i + 1])
        copy.start()
        pt_copies.append(copy)
    c_copy.wait()
    for b in range(blocks):
        c0, c1 = c_vmem[0, b], c_vmem[1, b]
        rhs[b, :NP, :LANES] = c0
        rhs[b, :NP, LANES:] = c1
        rhs[b, NP:, :LANES] = -c1
        rhs[b, NP:, LANES:] = c0
    out_copies = []
    for i, (first, size) in enumerate(parts):
        rows = pl.ds(first, size)
        pt_copies[i].wait()
        for b in range(blocks):
            cols = pl.ds(b * LANES, LANES)
            r = jnp.dot(pt_vmem[rows, :], rhs[b], preferred_element_type=jnp.float32)
            result[0, rows, cols] = r[:, :LANES].astype(result.dtype)
            result[1, rows, cols] = r[:, LANES:].astype(result.dtype)
        for k in range(2):
            copy = pltpu.make_async_copy(
                result.at[k, rows, :], out.at[k, rows, :], out_sem.at[i, k])
            copy.start()
            out_copies.append(copy)
    for copy in out_copies:
        copy.wait()


def spread_back(pt, coupled):
    depth = pt.shape[0]
    blocks = coupled.shape[1]
    parts = len(row_parts(depth))
    bf16 = jnp.bfloat16
    anywhere = pl.BlockSpec(memory_space=pl.ANY)
    return pl.pallas_call(
        spread_kernel,
        out_shape=jax.ShapeDtypeStruct((2, depth, blocks * LANES), bf16),
        in_specs=[anywhere, anywhere],
        out_specs=anywhere,
        scratch_shapes=[
            pltpu.VMEM(pt.shape, bf16),
            pltpu.VMEM(coupled.shape, bf16),
            pltpu.VMEM((blocks, 2 * NP, 2 * LANES), bf16),
            pltpu.VMEM((2, depth, blocks * LANES), bf16),
            pltpu.SemaphoreType.DMA((1 + parts,)),
            pltpu.SemaphoreType.DMA((parts, 2)),
        ],
        compiler_params=pltpu.CompilerParams(vmem_limit_bytes=60 * 2**20),
        name="spread_back",
    )(pt, coupled)


def solution(mesh):
    n_pw, n_band = mesh.shape["pw"], mesh.shape["band"]

    def shards(waves, projectors, coupling, offsets, counts):
        pt, coupled = gather_coupled(n_pw, n_band, waves, projectors, coupling, offsets, counts)
        return spread_back(pt, coupled)

    placed = (P(None, "pw", "band"), P(None, "band", "pw"), P(), P(), P())
    return jax.shard_map(
        shards, mesh=mesh, in_specs=placed, out_specs=P(None, "pw", "band"), check_vma=False
    )
```

```python
import functools

import jax
import jax.numpy as jnp
from jax import lax
from jax.experimental import pallas as pl
from jax.experimental.pallas import tpu as pltpu
from jax.sharding import PartitionSpec as P

NP = 128
M = 13
LANES = 128
SLOT = 16
SHIFT = 4
MESH = pl.DeviceIdType.MESH


def coupling_block(coupling, offsets, counts, spare):
    atoms, most, _ = coupling.shape
    wide = spare.shape[0]
    spare[...] = jnp.zeros_like(spare)
    for a in range(atoms):
        spare[a * SLOT:a * SLOT + most, :most] = coupling[a]

    def iota(shape, dim):
        return lax.broadcasted_iota(jnp.int32, shape, dim)

    place = iota((NP, wide), 1)
    atom, entry = place >> SHIFT, place & (SLOT - 1)
    start = jnp.full((NP, wide), -wide, jnp.int32)
    count = jnp.zeros((NP, wide), jnp.int32)
    for a in range(atoms):
        start = jnp.where(atom == a, offsets[a], start)
        count = jnp.where(atom == a, counts[a], count)
    select = jnp.where((iota((NP, wide), 0) == start + entry) & (entry < count), 1.0, 0.0)
    repeat = jnp.where((iota((LANES, wide), 1) & (SLOT - 1)) == iota((LANES, wide), 0), 1.0, 0.0)
    same = (iota((wide, wide), 0) >> SHIFT) == (iota((wide, wide), 1) >> SHIFT)
    spread = dot_exact(spare[...], repeat, 0)
    spread = jnp.where(same, spread, 0.0)
    raw = dot_exact(dot_exact(select, spread, 0), select, 1)
    return (raw + raw.T) * 0.5


def dot_exact(a, b, dim):
    return lax.dot_general(a, b, (((1,), (dim,)), ((), ())), precision=lax.Precision.HIGHEST,
                           preferred_element_type=jnp.float32)


def column_tiles(columns):
    return [(start, min(256, columns - start)) for start in range(0, columns, 256)]


def pieces_of(n_band, held):
    return [held - SLOT, SLOT] if n_band == 2 and held > SLOT else [held]


def windows_of(n_band, held):
    sizes = pieces_of(n_band, held)
    if n_band != 2 or held <= SLOT:
        return [None] * ((n_band - 1) * len(sizes)) + [(0, NP)]
    ends = [held - SLOT] + [held + sum(sizes[:s + 1]) - SLOT for s in range(len(sizes))]
    ends[-1] = NP
    return [(first, end - first) for first, end in zip([0] + ends[:-1], ends)]


def gather_kernel(n_pw, n_band, waves, proj, coupling_in, offsets_in, counts_in, pt_out, c_out,
                  w, p_all, acc, sib, send, recv, last_send, last_recv, total, c_all, pt, spare, block,
                  coupling, offsets, counts, small_sem, w_sem, own_sem, out_sem, p_send, p_recv, s_send, s_recv,
                  r_send, r_recv, l_send, l_recv, g_send, g_recv, f_send, f_recv, h_send, h_recv):
    pw = lax.axis_index("pw")
    band = lax.axis_index("band")
    chip, core = lax.div(pw, 2), lax.rem(pw, 2)
    chips = n_pw // 2
    held = proj.shape[1]
    columns = waves.shape[2]
    blocks = columns // LANES
    sizes = pieces_of(n_band, held)
    tiles = column_tiles(columns)
    sibling = (chip * 2 + 1 - core, band)
    windows = windows_of(n_band, held)
    bf16 = jnp.bfloat16

    def chip_at(step):
        return lax.rem(chip + step, chips)

    def pw_at(step):
        return lax.rem(pw + step, n_pw)

    def same_core(other):
        return (other * 2 + core, band)

    def sub_row(sender, s):
        if n_band != 2:
            return 0
        first = sum(sizes[:s])
        return pl.multiple_of(first + (1 - sender) * (held - 2 * first - sizes[s]), SLOT)

    def window(i):
        first, size = windows[i]
        if first == 0 and size == NP:
            return pl.ds(0, NP)
        return pl.ds(pl.multiple_of(first + band * (NP - 2 * first - size), SLOT), size)

    own_rows = pl.multiple_of(band * held, held)
    own = pltpu.make_async_copy(proj, p_all.at[:, pl.ds(own_rows, held), :], own_sem.at[0])
    own.start()
    small = [pltpu.make_async_copy(source, target, small_sem.at[i]) for i, (source, target) in enumerate(
        [(coupling_in, coupling), (offsets_in, offsets), (counts_in, counts)])]
    for copy in small:
        copy.start()
    wave_copies = []
    for t, (start, size) in enumerate(tiles):
        copy = pltpu.make_async_copy(
            waves.at[:, :, pl.ds(start, size)], w.at[:, :, pl.ds(start, size)], w_sem.at[t])
        copy.start()
        wave_copies.append(copy)

    barrier = pltpu.get_barrier_semaphore()
    for d in range(1, n_pw):
        pl.semaphore_signal(barrier, inc=1, device_id=(pw_at(d), band), device_id_type=MESH)
    for d in range(1, n_band):
        pl.semaphore_signal(barrier, inc=1, device_id=(pw, lax.rem(band + d, n_band)), device_id_type=MESH)
    for copy in small:
        copy.wait()
    block[...] = coupling_block(coupling, offsets, counts, spare)
    total[...] = jnp.zeros_like(total)
    pl.semaphore_wait(barrier, n_band - 1 + n_pw - 1)

    p_copies = []
    for d in range(1, n_band):
        for s, size in enumerate(sizes):
            row = sub_row(band, s)
            copy = pltpu.make_async_remote_copy(
                src_ref=proj.at[:, pl.ds(row, size), :],
                dst_ref=p_all.at[:, pl.ds(pl.multiple_of(own_rows + row, SLOT), size), :],
                send_sem=p_send.at[d - 1, s], recv_sem=p_recv.at[d - 1, s],
                device_id=(pw, lax.rem(band + d, n_band)), device_id_type=MESH)
            copy.start()
            p_copies.append(copy)

    pieces = [(own_rows, held)]
    for d in range(1, n_band):
        source = lax.rem(band + n_band - d, n_band)
        for s, size in enumerate(sizes):
            pieces.append((pl.multiple_of(source * held + sub_row(source, s), SLOT), size))
    last = len(pieces) - 1

    def project(i):
        row, size = pieces[i]
        rows = pl.ds(row, size)
        p0, p1 = p_all[0, rows, :], p_all[1, rows, :]
        lhs0 = jnp.concatenate([p0, -p1], axis=0)
        lhs1 = jnp.concatenate([p1, p0], axis=0)
        for t, (start, width) in enumerate(tiles):
            if i == 0:
                wave_copies[t].wait()
            cols = pl.ds(start, width)
            r = jnp.dot(lhs0, w[0, :, cols], preferred_element_type=jnp.float32)
            r += jnp.dot(lhs1, w[1, :, cols], preferred_element_type=jnp.float32)
            if i == last:
                for c in range(0, width, LANES):
                    last_send[0, (start + c) // LANES] = r[:size, c:c + LANES].astype(bf16)
                    last_send[1, (start + c) // LANES] = r[size:, c:c + LANES].astype(bf16)
            else:
                acc[0, rows, cols] = r[:size]
                acc[1, rows, cols] = r[size:]

    def sibling_copy(i):
        rows = pl.ds(*pieces[i])
        return pltpu.make_async_remote_copy(
            src_ref=acc.at[1 - core, rows, :], dst_ref=sib.at[rows, :],
            send_sem=s_send.at[i], recv_sem=s_recv.at[i],
            device_id=sibling, device_id_type=MESH)

    def reduce_copy(i, d):
        other = chip_at(d)
        rows = pl.ds(*pieces[i])
        return pltpu.make_async_remote_copy(
            src_ref=send.at[lax.min(other, blocks - 1), rows, :],
            dst_ref=recv.at[chip, rows, :],
            send_sem=r_send.at[i, d], recv_sem=r_recv.at[i, chip],
            device_id=same_core(other), device_id_type=MESH)

    def reduce_send(i):
        rows = pl.ds(*pieces[i])
        sibling_copy(i).wait_recv()
        for b in range(blocks):
            cols = pl.ds(b * LANES, LANES)
            send[b, rows, :] = (acc[core, rows, cols] + sib[rows, cols]).astype(bf16)
        for d in range(1, chips):
            pl.when(chip_at(d) < blocks)(lambda: reduce_copy(i, d).start())

    def last_copy(e):
        target = pw_at(e)
        return pltpu.make_async_remote_copy(
            src_ref=last_send.at[lax.rem(target, 2), lax.min(lax.div(target, 2), blocks - 1)],
            dst_ref=last_recv.at[pw],
            send_sem=l_send.at[e], recv_sem=l_recv.at[pw],
            device_id=(target, band), device_id_type=MESH)

    def gather_copy(i, b, d):
        rows = window(i)
        return pltpu.make_async_remote_copy(
            src_ref=c_all.at[core, b, rows, :], dst_ref=c_all.at[core, b, rows, :],
            send_sem=g_send.at[i, d], recv_sem=g_recv.at[i, b],
            device_id=same_core(chip_at(d)), device_id_type=MESH)

    def forward_copy(i, k, b):
        rows = window(i)
        return pltpu.make_async_remote_copy(
            src_ref=c_all.at[k, b, rows, :], dst_ref=c_all.at[k, b, rows, :],
            send_sem=f_send.at[i, b], recv_sem=f_recv.at[i, b],
            device_id=sibling, device_id_type=MESH)

    def final_copy(owner, e):
        here = c_all.at[lax.rem(owner, 2), lax.min(lax.div(owner, 2), blocks - 1), window(last), :]
        return pltpu.make_async_remote_copy(
            src_ref=here, dst_ref=here, send_sem=h_send.at[e], recv_sem=h_recv.at[owner],
            device_id=(pw_at(e), band), device_id_type=MESH)

    def couple(i):
        rows = pl.ds(*pieces[i])
        if i == last:
            value = last_send[core, chip].astype(jnp.float32)
            for e in range(1, n_pw):
                source = pw_at(e)
                pltpu.make_async_remote_copy(
                    src_ref=last_send.at[0, 0], dst_ref=last_recv.at[source],
                    send_sem=l_send.at[e], recv_sem=l_recv.at[source],
                    device_id=(source, band), device_id_type=MESH).wait_recv()
                value += last_recv[source].astype(jnp.float32)
        else:
            value = send[chip, rows, :].astype(jnp.float32)
            for d in range(1, chips):
                source = chip_at(d)
                pltpu.make_async_remote_copy(
                    src_ref=send.at[0, rows, :], dst_ref=recv.at[source, rows, :],
                    send_sem=r_send.at[i, d], recv_sem=r_recv.at[i, source],
                    device_id=same_core(source), device_id_type=MESH).wait_recv()
                value += recv[source, rows, :].astype(jnp.float32)
        total[rows, :] = value
        if windows[i] is None:
            return
        c_all[core, chip, window(i), :] = dot_exact(block[window(i), :], total[...], 0).astype(bf16)
        if i == last:
            for e in range(1, n_pw):
                final_copy(pw, e).start()
        else:
            for d in range(1, chips):
                gather_copy(i, chip, d).start()
            forward_copy(i, core, chip).start()

    def forward(i):
        for d in range(1, chips):
            source = chip_at(d)

            @pl.when(source < blocks)
            def _():
                gather_copy(i, source, d).wait_recv()
                forward_copy(i, core, source).start()

    def out_copy(i):
        rows = window(i)
        return pltpu.make_async_copy(
            c_all.at[:, :, rows, :], c_out.at[:, :, rows, :], out_sem.at[i + 1])

    early = [i for i in range(last) if windows[i] is not None]
    owns = chip < blocks

    own.wait()
    project(0)
    if last > 0:
        sibling_copy(0).start()
        reduce_send(0)
    for i in range(1, last + 1):
        p_copies[i - 1].wait_recv()
        project(i)
        if i < last:
            sibling_copy(i).start()
            reduce_send(i)
    for e in range(1, n_pw):
        pl.when(lax.div(pw_at(e), 2) < blocks)(lambda: last_copy(e).start())

    for i in range(last):
        pl.when(owns)(lambda: couple(i))

    pt[:, :NP] = p_all[0].T
    pt[:, NP:] = p_all[1].T
    pt_copy = pltpu.make_async_copy(pt, pt_out, out_sem.at[0])
    pt_copy.start()

    pl.when(owns)(lambda: couple(last))
    for i in early:
        forward(i)
    for i in early:
        for b in range(blocks):
            forward_copy(i, 1 - core, b).wait_recv()
        out_copy(i).start()
    for copy in p_copies:
        copy.wait_send()
    for i in range(last):
        sibling_copy(i).wait_send()
        for d in range(1, chips):
            pl.when(chip_at(d) < blocks)(lambda: reduce_copy(i, d).wait_send())
    for e in range(1, n_pw):
        pl.when(lax.div(pw_at(e), 2) < blocks)(lambda: final_copy(pw_at(e), e).wait_recv())
    out_copy(last).start()

    for e in range(1, n_pw):
        pl.when(lax.div(pw_at(e), 2) < blocks)(lambda: last_copy(e).wait_send())

    @pl.when(owns)
    def _():
        for i in early:
            for d in range(1, chips):
                gather_copy(i, chip, d).wait_send()
        for e in range(1, n_pw):
            final_copy(pw, e).wait_send()
    for i in early:
        for b in range(blocks):
            forward_copy(i, core, b).wait_send()
        out_copy(i).wait()
    pt_copy.wait()
    out_copy(last).wait()


def gather_coupled(n_pw, n_band, waves, projectors, coupling, offsets, counts):
    _, depth, columns = waves.shape
    held = projectors.shape[1]
    chips = n_pw // 2
    blocks = columns // LANES
    sizes = pieces_of(n_band, held)
    subs = len(sizes)
    pieces = 1 + (n_band - 1) * subs
    last_rows = sizes[-1]
    bf16, f32 = jnp.bfloat16, jnp.float32
    dma = pltpu.SemaphoreType.DMA
    anywhere = pl.BlockSpec(memory_space=pl.ANY)
    wide = -(-coupling.shape[0] * SLOT // LANES) * LANES
    return pl.pallas_call(
        functools.partial(gather_kernel, n_pw, n_band),
        out_shape=[
            jax.ShapeDtypeStruct((depth, 2 * NP), bf16),
            jax.ShapeDtypeStruct((2, blocks, NP, LANES), bf16),
        ],
        in_specs=[anywhere] * 5,
        out_specs=[anywhere, anywhere],
        scratch_shapes=[
            pltpu.VMEM((2, depth, columns), bf16),
            pltpu.VMEM((2, NP, depth), bf16),
            pltpu.VMEM((2, NP, columns), f32),
            pltpu.VMEM((NP, columns), f32),
            pltpu.VMEM((blocks, NP, LANES), bf16),
            pltpu.VMEM((chips, NP, LANES), bf16),
            pltpu.VMEM((2, blocks, last_rows, LANES), bf16),
            pltpu.VMEM((n_pw, last_rows, LANES), bf16),
            pltpu.VMEM((NP, LANES), f32),
            pltpu.VMEM((2, blocks, NP, LANES), bf16),
            pltpu.VMEM((depth, 2 * NP), bf16),
            pltpu.VMEM((wide, LANES), f32),
            pltpu.VMEM((NP, NP), f32),
            pltpu.VMEM(coupling.shape, f32),
            pltpu.SMEM(offsets.shape, jnp.int32),
            pltpu.SMEM(counts.shape, jnp.int32),
            dma((3,)),
            dma((len(column_tiles(columns)),)), dma((1,)), dma((1 + pieces,)),
            dma((n_band - 1, subs)), dma((n_band - 1, subs)),
            dma((pieces,)), dma((pieces,)),
            dma((pieces, chips)), dma((pieces, chips)),
            dma((n_pw,)), dma((n_pw,)),
            dma((pieces, chips)), dma((pieces, blocks)),
            dma((pieces, blocks)), dma((pieces, blocks)),
            dma((n_pw,)), dma((n_pw,)),
        ],
        compiler_params=pltpu.CompilerParams(
            collective_id=0, has_side_effects=True, vmem_limit_bytes=60 * 2**20),
        name="gather_coupled",
    )(waves, projectors, coupling, offsets, counts)


def row_parts(depth):
    ends = list(range(768, depth, 768)) + [depth]
    return [(first, end - first) for first, end in zip([0] + ends[:-1], ends)]


def spread_kernel(pt, c, out, pt_vmem, c_vmem, rhs, result, in_sem, out_sem):
    blocks = c.shape[1]
    parts = row_parts(pt.shape[0])
    c_copy = pltpu.make_async_copy(c, c_vmem, in_sem.at[0])
    c_copy.start()
    pt_copies = []
    for i, (first, size) in enumerate(parts):
        rows = pl.ds(first, size)
        copy = pltpu.make_async_copy(pt.at[rows, :], pt_vmem.at[rows, :], in_sem.at[i + 1])
        copy.start()
        pt_copies.append(copy)
    c_copy.wait()
    for b in range(blocks):
        c0, c1 = c_vmem[0, b], c_vmem[1, b]
        rhs[b, :NP, :LANES] = c0
        rhs[b, :NP, LANES:] = c1
        rhs[b, NP:, :LANES] = -c1
        rhs[b, NP:, LANES:] = c0
    out_copies = []
    for i, (first, size) in enumerate(parts):
        rows = pl.ds(first, size)
        pt_copies[i].wait()
        for b in range(blocks):
            cols = pl.ds(b * LANES, LANES)
            r = jnp.dot(pt_vmem[rows, :], rhs[b], preferred_element_type=jnp.float32)
            result[0, rows, cols] = r[:, :LANES].astype(result.dtype)
            result[1, rows, cols] = r[:, LANES:].astype(result.dtype)
        for k in range(2):
            copy = pltpu.make_async_copy(
                result.at[k, rows, :], out.at[k, rows, :], out_sem.at[i, k])
            copy.start()
            out_copies.append(copy)
    for copy in out_copies:
        copy.wait()


def spread_back(pt, coupled):
    depth = pt.shape[0]
    blocks = coupled.shape[1]
    parts = len(row_parts(depth))
    bf16 = jnp.bfloat16
    anywhere = pl.BlockSpec(memory_space=pl.ANY)
    return pl.pallas_call(
        spread_kernel,
        out_shape=jax.ShapeDtypeStruct((2, depth, blocks * LANES), bf16),
        in_specs=[anywhere, anywhere],
        out_specs=anywhere,
        scratch_shapes=[
            pltpu.VMEM(pt.shape, bf16),
            pltpu.VMEM(coupled.shape, bf16),
            pltpu.VMEM((blocks, 2 * NP, 2 * LANES), bf16),
            pltpu.VMEM((2, depth, blocks * LANES), bf16),
            pltpu.SemaphoreType.DMA((1 + parts,)),
            pltpu.SemaphoreType.DMA((parts, 2)),
        ],
        compiler_params=pltpu.CompilerParams(vmem_limit_bytes=60 * 2**20),
        name="spread_back",
    )(pt, coupled)


def solution(mesh):
    n_pw, n_band = mesh.shape["pw"], mesh.shape["band"]

    def shards(waves, projectors, coupling, offsets, counts):
        pt, coupled = gather_coupled(n_pw, n_band, waves, projectors, coupling, offsets, counts)
        return spread_back(pt, coupled)

    placed = (P(None, "pw", "band"), P(None, "band", "pw"), P(), P(), P())
    return jax.shard_map(
        shards, mesh=mesh, in_specs=placed, out_specs=P(None, "pw", "band"), check_vma=False
    )
```

```python
import functools

import jax
import jax.numpy as jnp
from jax import lax
from jax.experimental import pallas as pl
from jax.experimental.pallas import tpu as pltpu
from jax.sharding import PartitionSpec as P

NP = 128
M = 13
LANES = 128
SLOT = 16
SHIFT = 4
MESH = pl.DeviceIdType.MESH


def coupling_block(coupling, offsets, counts, spare):
    atoms, most, _ = coupling.shape
    wide = spare.shape[0]
    spare[...] = jnp.zeros_like(spare)
    for a in range(atoms):
        spare[a * SLOT:a * SLOT + most, :most] = coupling[a]

    def iota(shape, dim):
        return lax.broadcasted_iota(jnp.int32, shape, dim)

    place = iota((NP, wide), 1)
    atom, entry = place >> SHIFT, place & (SLOT - 1)
    start = jnp.full((NP, wide), -wide, jnp.int32)
    count = jnp.zeros((NP, wide), jnp.int32)
    for a in range(atoms):
        start = jnp.where(atom == a, offsets[a], start)
        count = jnp.where(atom == a, counts[a], count)
    select = jnp.where((iota((NP, wide), 0) == start + entry) & (entry < count), 1.0, 0.0)
    repeat = jnp.where((iota((LANES, wide), 1) & (SLOT - 1)) == iota((LANES, wide), 0), 1.0, 0.0)
    same = (iota((wide, wide), 0) >> SHIFT) == (iota((wide, wide), 1) >> SHIFT)
    spread = dot_exact(spare[...], repeat, 0)
    spread = jnp.where(same, spread, 0.0)
    raw = dot_exact(dot_exact(select, spread, 0), select, 1)
    return (raw + raw.T) * 0.5


def dot_exact(a, b, dim):
    return lax.dot_general(a, b, (((1,), (dim,)), ((), ())), precision=lax.Precision.HIGHEST,
                           preferred_element_type=jnp.float32)


def column_tiles(columns):
    return [(start, min(256, columns - start)) for start in range(0, columns, 256)]


def pieces_of(n_band, held):
    return [held - SLOT, SLOT] if n_band == 2 and held > SLOT else [held]


def windows_of(n_band, held):
    sizes = pieces_of(n_band, held)
    if n_band != 2 or held <= SLOT:
        return [None] * ((n_band - 1) * len(sizes)) + [(0, NP)]
    ends = [held - SLOT] + [held + sum(sizes[:s + 1]) - SLOT for s in range(len(sizes))]
    ends[-1] = NP
    return [(first, end - first) for first, end in zip([0] + ends[:-1], ends)]


def gather_kernel(n_pw, n_band, waves, proj, coupling_in, offsets_in, counts_in, pt_out, c_out,
                  w, p_all, acc, sib, send, recv, last_send, last_recv, total, c_all, pt, spare, block,
                  coupling, offsets, counts, small_sem, w_sem, own_sem, out_sem, p_send, p_recv, s_send, s_recv,
                  r_send, r_recv, l_send, l_recv, g_send, g_recv, y_send, f_send, f_recv, h_send, h_recv):
    pw = lax.axis_index("pw")
    band = lax.axis_index("band")
    chip, core = lax.div(pw, 2), lax.rem(pw, 2)
    chips = n_pw // 2
    held = proj.shape[1]
    columns = waves.shape[2]
    blocks = columns // LANES
    sizes = pieces_of(n_band, held)
    tiles = column_tiles(columns)
    sibling = (chip * 2 + 1 - core, band)
    windows = windows_of(n_band, held)
    bf16 = jnp.bfloat16

    def chip_at(step):
        return lax.rem(chip + step, chips)

    def pw_at(step):
        return lax.rem(pw + step, n_pw)

    side = 4 if chips % 4 == 0 else 1
    across = chips // side

    def chip_of(dz, dy):
        z, y = lax.div(chip, across), lax.rem(chip, across)
        return lax.rem(z + dz, side) * across + lax.rem(y + dy, across)

    def same_core(other):
        return (other * 2 + core, band)

    def sub_row(sender, s):
        if n_band != 2:
            return 0
        first = sum(sizes[:s])
        return pl.multiple_of(first + (1 - sender) * (held - 2 * first - sizes[s]), SLOT)

    def window(i):
        first, size = windows[i]
        if first == 0 and size == NP:
            return pl.ds(0, NP)
        return pl.ds(pl.multiple_of(first + band * (NP - 2 * first - size), SLOT), size)

    own_rows = pl.multiple_of(band * held, held)
    own = pltpu.make_async_copy(proj, p_all.at[:, pl.ds(own_rows, held), :], own_sem.at[0])
    own.start()
    small = [pltpu.make_async_copy(source, target, small_sem.at[i]) for i, (source, target) in enumerate(
        [(coupling_in, coupling), (offsets_in, offsets), (counts_in, counts)])]
    for copy in small:
        copy.start()
    wave_copies = []
    for t, (start, size) in enumerate(tiles):
        copy = pltpu.make_async_copy(
            waves.at[:, :, pl.ds(start, size)], w.at[:, :, pl.ds(start, size)], w_sem.at[t])
        copy.start()
        wave_copies.append(copy)

    barrier = pltpu.get_barrier_semaphore()
    for d in range(1, n_pw):
        pl.semaphore_signal(barrier, inc=1, device_id=(pw_at(d), band), device_id_type=MESH)
    for d in range(1, n_band):
        pl.semaphore_signal(barrier, inc=1, device_id=(pw, lax.rem(band + d, n_band)), device_id_type=MESH)
    for copy in small:
        copy.wait()
    block[...] = coupling_block(coupling, offsets, counts, spare)
    total[...] = jnp.zeros_like(total)
    pl.semaphore_wait(barrier, n_band - 1 + n_pw - 1)

    p_copies = []
    for d in range(1, n_band):
        for s, size in enumerate(sizes):
            row = sub_row(band, s)
            copy = pltpu.make_async_remote_copy(
                src_ref=proj.at[:, pl.ds(row, size), :],
                dst_ref=p_all.at[:, pl.ds(pl.multiple_of(own_rows + row, SLOT), size), :],
                send_sem=p_send.at[d - 1, s], recv_sem=p_recv.at[d - 1, s],
                device_id=(pw, lax.rem(band + d, n_band)), device_id_type=MESH)
            copy.start()
            p_copies.append(copy)

    pieces = [(own_rows, held)]
    for d in range(1, n_band):
        source = lax.rem(band + n_band - d, n_band)
        for s, size in enumerate(sizes):
            pieces.append((pl.multiple_of(source * held + sub_row(source, s), SLOT), size))
    last = len(pieces) - 1

    def project(i):
        row, size = pieces[i]
        rows = pl.ds(row, size)
        p0, p1 = p_all[0, rows, :], p_all[1, rows, :]
        lhs0 = jnp.concatenate([p0, -p1], axis=0)
        lhs1 = jnp.concatenate([p1, p0], axis=0)
        for t, (start, width) in enumerate(tiles):
            if i == 0:
                wave_copies[t].wait()
            cols = pl.ds(start, width)
            r = jnp.dot(lhs0, w[0, :, cols], preferred_element_type=jnp.float32)
            r += jnp.dot(lhs1, w[1, :, cols], preferred_element_type=jnp.float32)
            if i == last:
                for c in range(0, width, LANES):
                    last_send[0, (start + c) // LANES] = r[:size, c:c + LANES].astype(bf16)
                    last_send[1, (start + c) // LANES] = r[size:, c:c + LANES].astype(bf16)
            else:
                acc[0, rows, cols] = r[:size]
                acc[1, rows, cols] = r[size:]

    def sibling_copy(i):
        rows = pl.ds(*pieces[i])
        return pltpu.make_async_remote_copy(
            src_ref=acc.at[1 - core, rows, :], dst_ref=sib.at[rows, :],
            send_sem=s_send.at[i], recv_sem=s_recv.at[i],
            device_id=sibling, device_id_type=MESH)

    def reduce_copy(i, d):
        other = chip_at(d)
        rows = pl.ds(*pieces[i])
        return pltpu.make_async_remote_copy(
            src_ref=send.at[lax.min(other, blocks - 1), rows, :],
            dst_ref=recv.at[chip, rows, :],
            send_sem=r_send.at[i, d], recv_sem=r_recv.at[i, chip],
            device_id=same_core(other), device_id_type=MESH)

    def reduce_send(i):
        rows = pl.ds(*pieces[i])
        sibling_copy(i).wait_recv()
        for b in range(blocks):
            cols = pl.ds(b * LANES, LANES)
            send[b, rows, :] = (acc[core, rows, cols] + sib[rows, cols]).astype(bf16)
        for d in range(1, chips):
            pl.when(chip_at(d) < blocks)(lambda: reduce_copy(i, d).start())

    def last_copy(e):
        target = pw_at(e)
        return pltpu.make_async_remote_copy(
            src_ref=last_send.at[lax.rem(target, 2), lax.min(lax.div(target, 2), blocks - 1)],
            dst_ref=last_recv.at[pw],
            send_sem=l_send.at[e], recv_sem=l_recv.at[pw],
            device_id=(target, band), device_id_type=MESH)

    def line_copy(i, b, dz):
        rows = window(i)
        return pltpu.make_async_remote_copy(
            src_ref=c_all.at[core, b, rows, :], dst_ref=c_all.at[core, b, rows, :],
            send_sem=g_send.at[i, dz], recv_sem=g_recv.at[i, b],
            device_id=same_core(chip_of(dz, 0)), device_id_type=MESH)

    def cross_copy(i, b, dy):
        rows = window(i)
        return pltpu.make_async_remote_copy(
            src_ref=c_all.at[core, b, rows, :], dst_ref=c_all.at[core, b, rows, :],
            send_sem=y_send.at[i, b, dy], recv_sem=g_recv.at[i, b],
            device_id=same_core(chip_of(0, dy)), device_id_type=MESH)

    def forward_copy(i, k, b):
        rows = window(i)
        return pltpu.make_async_remote_copy(
            src_ref=c_all.at[k, b, rows, :], dst_ref=c_all.at[k, b, rows, :],
            send_sem=f_send.at[i, b], recv_sem=f_recv.at[i, b],
            device_id=sibling, device_id_type=MESH)

    def final_copy(owner, e):
        here = c_all.at[lax.rem(owner, 2), lax.min(lax.div(owner, 2), blocks - 1), window(last), :]
        return pltpu.make_async_remote_copy(
            src_ref=here, dst_ref=here, send_sem=h_send.at[e], recv_sem=h_recv.at[owner],
            device_id=(pw_at(e), band), device_id_type=MESH)

    def couple(i):
        rows = pl.ds(*pieces[i])
        if i == last:
            value = last_send[core, chip].astype(jnp.float32)
            for e in range(1, n_pw):
                source = pw_at(e)
                pltpu.make_async_remote_copy(
                    src_ref=last_send.at[0, 0], dst_ref=last_recv.at[source],
                    send_sem=l_send.at[e], recv_sem=l_recv.at[source],
                    device_id=(source, band), device_id_type=MESH).wait_recv()
                value += last_recv[source].astype(jnp.float32)
        else:
            value = send[chip, rows, :].astype(jnp.float32)
            for d in range(1, chips):
                source = chip_at(d)
                pltpu.make_async_remote_copy(
                    src_ref=send.at[0, rows, :], dst_ref=recv.at[source, rows, :],
                    send_sem=r_send.at[i, d], recv_sem=r_recv.at[i, source],
                    device_id=same_core(source), device_id_type=MESH).wait_recv()
                value += recv[source, rows, :].astype(jnp.float32)
        total[rows, :] = value
        if windows[i] is None:
            return
        c_all[core, chip, window(i), :] = dot_exact(block[window(i), :], total[...], 0).astype(bf16)
        if i == last:
            for e in range(1, n_pw):
                final_copy(pw, e).start()
        else:
            for dz in range(1, side):
                line_copy(i, chip, dz).start()
            for dy in range(1, across):
                cross_copy(i, chip, dy).start()
            forward_copy(i, core, chip).start()

    def forward_line(i):
        for dz in range(1, side):
            source = chip_of(dz, 0)

            @pl.when(source < blocks)
            def _():
                line_copy(i, source, dz).wait_recv()
                for dy in range(1, across):
                    cross_copy(i, source, dy).start()
                forward_copy(i, core, source).start()

    def forward_cross(i):
        for dz in range(side):
            for dy in range(1, across):
                source = chip_of(dz, dy)

                @pl.when(source < blocks)
                def _():
                    cross_copy(i, source, dy).wait_recv()
                    forward_copy(i, core, source).start()

    def out_copy(i):
        rows = window(i)
        return pltpu.make_async_copy(
            c_all.at[:, :, rows, :], c_out.at[:, :, rows, :], out_sem.at[i + 1])

    early = [i for i in range(last) if windows[i] is not None]
    owns = chip < blocks

    own.wait()
    project(0)
    if last > 0:
        sibling_copy(0).start()
        reduce_send(0)
    for i in range(1, last + 1):
        p_copies[i - 1].wait_recv()
        project(i)
        if i < last:
            sibling_copy(i).start()
            reduce_send(i)
    for e in range(1, n_pw):
        pl.when(lax.div(pw_at(e), 2) < blocks)(lambda: last_copy(e).start())

    for i in range(last):
        pl.when(owns)(lambda: couple(i))

    pt[:, :NP] = p_all[0].T
    pt[:, NP:] = p_all[1].T
    pt_copy = pltpu.make_async_copy(pt, pt_out, out_sem.at[0])
    pt_copy.start()

    pl.when(owns)(lambda: couple(last))
    for i in early:
        forward_line(i)
    for i in early:
        forward_cross(i)
    for i in early:
        for b in range(blocks):
            forward_copy(i, 1 - core, b).wait_recv()
        out_copy(i).start()
    for copy in p_copies:
        copy.wait_send()
    for i in range(last):
        sibling_copy(i).wait_send()
        for d in range(1, chips):
            pl.when(chip_at(d) < blocks)(lambda: reduce_copy(i, d).wait_send())
    for e in range(1, n_pw):
        pl.when(lax.div(pw_at(e), 2) < blocks)(lambda: final_copy(pw_at(e), e).wait_recv())
    out_copy(last).start()

    for e in range(1, n_pw):
        pl.when(lax.div(pw_at(e), 2) < blocks)(lambda: last_copy(e).wait_send())

    @pl.when(owns)
    def _():
        for i in early:
            for dz in range(1, side):
                line_copy(i, chip, dz).wait_send()
            for dy in range(1, across):
                cross_copy(i, chip, dy).wait_send()
        for e in range(1, n_pw):
            final_copy(pw, e).wait_send()
    for i in early:
        for b in range(blocks):
            forward_copy(i, core, b).wait_send()
        for dz in range(1, side):
            source = chip_of(dz, 0)
            for dy in range(1, across):
                pl.when(source < blocks)(lambda: cross_copy(i, source, dy).wait_send())
        out_copy(i).wait()
    pt_copy.wait()
    out_copy(last).wait()


def gather_coupled(n_pw, n_band, waves, projectors, coupling, offsets, counts):
    _, depth, columns = waves.shape
    held = projectors.shape[1]
    chips = n_pw // 2
    blocks = columns // LANES
    sizes = pieces_of(n_band, held)
    subs = len(sizes)
    pieces = 1 + (n_band - 1) * subs
    last_rows = sizes[-1]
    bf16, f32 = jnp.bfloat16, jnp.float32
    dma = pltpu.SemaphoreType.DMA
    anywhere = pl.BlockSpec(memory_space=pl.ANY)
    wide = -(-coupling.shape[0] * SLOT // LANES) * LANES
    return pl.pallas_call(
        functools.partial(gather_kernel, n_pw, n_band),
        out_shape=[
            jax.ShapeDtypeStruct((depth, 2 * NP), bf16),
            jax.ShapeDtypeStruct((2, blocks, NP, LANES), bf16),
        ],
        in_specs=[anywhere] * 5,
        out_specs=[anywhere, anywhere],
        scratch_shapes=[
            pltpu.VMEM((2, depth, columns), bf16),
            pltpu.VMEM((2, NP, depth), bf16),
            pltpu.VMEM((2, NP, columns), f32),
            pltpu.VMEM((NP, columns), f32),
            pltpu.VMEM((blocks, NP, LANES), bf16),
            pltpu.VMEM((chips, NP, LANES), bf16),
            pltpu.VMEM((2, blocks, last_rows, LANES), bf16),
            pltpu.VMEM((n_pw, last_rows, LANES), bf16),
            pltpu.VMEM((NP, LANES), f32),
            pltpu.VMEM((2, blocks, NP, LANES), bf16),
            pltpu.VMEM((depth, 2 * NP), bf16),
            pltpu.VMEM((wide, LANES), f32),
            pltpu.VMEM((NP, NP), f32),
            pltpu.VMEM(coupling.shape, f32),
            pltpu.SMEM(offsets.shape, jnp.int32),
            pltpu.SMEM(counts.shape, jnp.int32),
            dma((3,)),
            dma((len(column_tiles(columns)),)), dma((1,)), dma((1 + pieces,)),
            dma((n_band - 1, subs)), dma((n_band - 1, subs)),
            dma((pieces,)), dma((pieces,)),
            dma((pieces, chips)), dma((pieces, chips)),
            dma((n_pw,)), dma((n_pw,)),
            dma((pieces, chips)), dma((pieces, blocks)), dma((pieces, blocks, chips)),
            dma((pieces, blocks)), dma((pieces, blocks)),
            dma((n_pw,)), dma((n_pw,)),
        ],
        compiler_params=pltpu.CompilerParams(
            collective_id=0, has_side_effects=True, vmem_limit_bytes=60 * 2**20),
        name="gather_coupled",
    )(waves, projectors, coupling, offsets, counts)


def row_parts(depth):
    ends = list(range(512, depth, 512)) + [depth]
    return [(first, end - first) for first, end in zip([0] + ends[:-1], ends)]


def spread_kernel(pt, c, out, pt_vmem, c_vmem, rhs, result, in_sem, out_sem):
    blocks = c.shape[1]
    parts = row_parts(pt.shape[0])
    c_copy = pltpu.make_async_copy(c, c_vmem, in_sem.at[0])
    c_copy.start()
    pt_copies = []
    for i, (first, size) in enumerate(parts):
        rows = pl.ds(first, size)
        copy = pltpu.make_async_copy(pt.at[rows, :], pt_vmem.at[rows, :], in_sem.at[i + 1])
        copy.start()
        pt_copies.append(copy)
    c_copy.wait()
    for b in range(blocks):
        c0, c1 = c_vmem[0, b], c_vmem[1, b]
        rhs[b, :NP, :LANES] = c0
        rhs[b, :NP, LANES:] = c1
        rhs[b, NP:, :LANES] = -c1
        rhs[b, NP:, LANES:] = c0
    out_copies = []
    for i, (first, size) in enumerate(parts):
        rows = pl.ds(first, size)
        pt_copies[i].wait()
        for b in range(blocks):
            cols = pl.ds(b * LANES, LANES)
            r = jnp.dot(pt_vmem[rows, :], rhs[b], preferred_element_type=jnp.float32)
            result[0, rows, cols] = r[:, :LANES].astype(result.dtype)
            result[1, rows, cols] = r[:, LANES:].astype(result.dtype)
        for k in range(2):
            copy = pltpu.make_async_copy(
                result.at[k, rows, :], out.at[k, rows, :], out_sem.at[i, k])
            copy.start()
            out_copies.append(copy)
    for copy in out_copies:
        copy.wait()


def spread_back(pt, coupled):
    depth = pt.shape[0]
    blocks = coupled.shape[1]
    parts = len(row_parts(depth))
    bf16 = jnp.bfloat16
    anywhere = pl.BlockSpec(memory_space=pl.ANY)
    return pl.pallas_call(
        spread_kernel,
        out_shape=jax.ShapeDtypeStruct((2, depth, blocks * LANES), bf16),
        in_specs=[anywhere, anywhere],
        out_specs=anywhere,
        scratch_shapes=[
            pltpu.VMEM(pt.shape, bf16),
            pltpu.VMEM(coupled.shape, bf16),
            pltpu.VMEM((blocks, 2 * NP, 2 * LANES), bf16),
            pltpu.VMEM((2, depth, blocks * LANES), bf16),
            pltpu.SemaphoreType.DMA((1 + parts,)),
            pltpu.SemaphoreType.DMA((parts, 2)),
        ],
        compiler_params=pltpu.CompilerParams(vmem_limit_bytes=60 * 2**20),
        name="spread_back",
    )(pt, coupled)


def solution(mesh):
    n_pw, n_band = mesh.shape["pw"], mesh.shape["band"]

    def shards(waves, projectors, coupling, offsets, counts):
        pt, coupled = gather_coupled(n_pw, n_band, waves, projectors, coupling, offsets, counts)
        return spread_back(pt, coupled)

    placed = (P(None, "pw", "band"), P(None, "band", "pw"), P(), P(), P())
    return jax.shard_map(
        shards, mesh=mesh, in_specs=placed, out_specs=P(None, "pw", "band"), check_vma=False
    )
```

```python
import functools

import jax
import jax.numpy as jnp
from jax import lax
from jax.experimental import pallas as pl
from jax.experimental.pallas import tpu as pltpu
from jax.sharding import PartitionSpec as P

NP = 128
M = 13
LANES = 128
SLOT = 16
SHIFT = 4
MESH = pl.DeviceIdType.MESH


def coupling_block(coupling, offsets, counts, spare):
    atoms, most, _ = coupling.shape
    wide = spare.shape[0]
    spare[...] = jnp.zeros_like(spare)
    for a in range(atoms):
        spare[a * SLOT:a * SLOT + most, :most] = coupling[a]

    def iota(shape, dim):
        return lax.broadcasted_iota(jnp.int32, shape, dim)

    place = iota((NP, wide), 1)
    atom, entry = place >> SHIFT, place & (SLOT - 1)
    start = jnp.full((NP, wide), -wide, jnp.int32)
    count = jnp.zeros((NP, wide), jnp.int32)
    for a in range(atoms):
        start = jnp.where(atom == a, offsets[a], start)
        count = jnp.where(atom == a, counts[a], count)
    select = jnp.where((iota((NP, wide), 0) == start + entry) & (entry < count), 1.0, 0.0)
    repeat = jnp.where((iota((LANES, wide), 1) & (SLOT - 1)) == iota((LANES, wide), 0), 1.0, 0.0)
    same = (iota((wide, wide), 0) >> SHIFT) == (iota((wide, wide), 1) >> SHIFT)
    spread = dot_exact(spare[...], repeat, 0)
    spread = jnp.where(same, spread, 0.0)
    raw = dot_exact(dot_exact(select, spread, 0), select, 1)
    return (raw + raw.T) * 0.5


def dot_exact(a, b, dim):
    return lax.dot_general(a, b, (((1,), (dim,)), ((), ())), precision=lax.Precision.HIGHEST,
                           preferred_element_type=jnp.float32)


def column_tiles(columns):
    return [(start, min(256, columns - start)) for start in range(0, columns, 256)]


def pieces_of(n_band, held):
    return [held - SLOT, SLOT] if n_band == 2 and held > SLOT else [held]


def windows_of(n_band, held):
    sizes = pieces_of(n_band, held)
    if n_band != 2 or held <= SLOT:
        return [None] * ((n_band - 1) * len(sizes)) + [(0, NP)]
    ends = [held - SLOT] + [held + sum(sizes[:s + 1]) - SLOT for s in range(len(sizes))]
    ends[-1] = NP
    return [(first, end - first) for first, end in zip([0] + ends[:-1], ends)]


def gather_kernel(n_pw, n_band, waves, proj, coupling_in, offsets_in, counts_in, pt_out, c_out,
                  w, p_all, acc, sib, send, recv, last_send, last_recv, total, c_all, pt, spare, block,
                  coupling, offsets, counts, small_sem, w_sem, own_sem, out_sem, p_send, p_recv, s_send, s_recv,
                  r_send, r_recv, l_send, l_recv, g_send, g_recv, f_send, f_recv, h_send, h_recv):
    pw = lax.axis_index("pw")
    band = lax.axis_index("band")
    chip, core = lax.div(pw, 2), lax.rem(pw, 2)
    chips = n_pw // 2
    held = proj.shape[1]
    columns = waves.shape[2]
    blocks = columns // LANES
    sizes = pieces_of(n_band, held)
    tiles = column_tiles(columns)
    sibling = (chip * 2 + 1 - core, band)
    windows = windows_of(n_band, held)
    bf16 = jnp.bfloat16

    def chip_at(step):
        return lax.rem(chip + step, chips)

    def pw_at(step):
        return lax.rem(pw + step, n_pw)

    def same_core(other):
        return (other * 2 + core, band)

    def sub_row(sender, s):
        if n_band != 2:
            return 0
        first = sum(sizes[:s])
        return pl.multiple_of(first + (1 - sender) * (held - 2 * first - sizes[s]), SLOT)

    def window(i):
        first, size = windows[i]
        if first == 0 and size == NP:
            return pl.ds(0, NP)
        return pl.ds(pl.multiple_of(first + band * (NP - 2 * first - size), SLOT), size)

    own_rows = pl.multiple_of(band * held, held)
    own = pltpu.make_async_copy(proj, p_all.at[:, pl.ds(own_rows, held), :], own_sem.at[0])
    own.start()
    small = [pltpu.make_async_copy(source, target, small_sem.at[i]) for i, (source, target) in enumerate(
        [(coupling_in, coupling), (offsets_in, offsets), (counts_in, counts)])]
    for copy in small:
        copy.start()
    wave_copies = []
    for t, (start, size) in enumerate(tiles):
        copy = pltpu.make_async_copy(
            waves.at[:, :, pl.ds(start, size)], w.at[:, :, pl.ds(start, size)], w_sem.at[t])
        copy.start()
        wave_copies.append(copy)

    barrier = pltpu.get_barrier_semaphore()
    for d in range(1, n_pw):
        pl.semaphore_signal(barrier, inc=1, device_id=(pw_at(d), band), device_id_type=MESH)
    for d in range(1, n_band):
        pl.semaphore_signal(barrier, inc=1, device_id=(pw, lax.rem(band + d, n_band)), device_id_type=MESH)
    for copy in small:
        copy.wait()
    block[...] = coupling_block(coupling, offsets, counts, spare)
    total[...] = jnp.zeros_like(total)
    pl.semaphore_wait(barrier, n_band - 1 + n_pw - 1)

    p_copies = []
    for d in range(1, n_band):
        for s, size in enumerate(sizes):
            row = sub_row(band, s)
            copy = pltpu.make_async_remote_copy(
                src_ref=proj.at[:, pl.ds(row, size), :],
                dst_ref=p_all.at[:, pl.ds(pl.multiple_of(own_rows + row, SLOT), size), :],
                send_sem=p_send.at[d - 1, s], recv_sem=p_recv.at[d - 1, s],
                device_id=(pw, lax.rem(band + d, n_band)), device_id_type=MESH)
            copy.start()
            p_copies.append(copy)

    pieces = [(own_rows, held)]
    for d in range(1, n_band):
        source = lax.rem(band + n_band - d, n_band)
        for s, size in enumerate(sizes):
            pieces.append((pl.multiple_of(source * held + sub_row(source, s), SLOT), size))
    last = len(pieces) - 1

    def project(i):
        row, size = pieces[i]
        rows = pl.ds(row, size)
        p0, p1 = p_all[0, rows, :], p_all[1, rows, :]
        lhs0 = jnp.concatenate([p0, -p1], axis=0)
        lhs1 = jnp.concatenate([p1, p0], axis=0)
        for t, (start, width) in enumerate(tiles):
            if i == 0:
                wave_copies[t].wait()
            cols = pl.ds(start, width)
            r = jnp.dot(lhs0, w[0, :, cols], preferred_element_type=jnp.float32)
            r += jnp.dot(lhs1, w[1, :, cols], preferred_element_type=jnp.float32)
            if i == last:
                for c in range(0, width, LANES):
                    last_send[0, (start + c) // LANES] = r[:size, c:c + LANES].astype(bf16)
                    last_send[1, (start + c) // LANES] = r[size:, c:c + LANES].astype(bf16)
            else:
                acc[0, rows, cols] = r[:size]
                acc[1, rows, cols] = r[size:]

    def sibling_copy(i):
        rows = pl.ds(*pieces[i])
        return pltpu.make_async_remote_copy(
            src_ref=acc.at[1 - core, rows, :], dst_ref=sib.at[rows, :],
            send_sem=s_send.at[i], recv_sem=s_recv.at[i],
            device_id=sibling, device_id_type=MESH)

    def reduce_copy(i, d):
        other = chip_at(d)
        rows = pl.ds(*pieces[i])
        return pltpu.make_async_remote_copy(
            src_ref=send.at[lax.min(other, blocks - 1), rows, :],
            dst_ref=recv.at[chip, rows, :],
            send_sem=r_send.at[i, d], recv_sem=r_recv.at[i, chip],
            device_id=same_core(other), device_id_type=MESH)

    def reduce_send(i):
        rows = pl.ds(*pieces[i])
        sibling_copy(i).wait_recv()
        for b in range(blocks):
            cols = pl.ds(b * LANES, LANES)
            send[b, rows, :] = (acc[core, rows, cols] + sib[rows, cols]).astype(bf16)
        for d in range(1, chips):
            pl.when(chip_at(d) < blocks)(lambda: reduce_copy(i, d).start())

    def last_copy(e):
        target = pw_at(e)
        return pltpu.make_async_remote_copy(
            src_ref=last_send.at[lax.rem(target, 2), lax.min(lax.div(target, 2), blocks - 1)],
            dst_ref=last_recv.at[pw],
            send_sem=l_send.at[e], recv_sem=l_recv.at[pw],
            device_id=(target, band), device_id_type=MESH)

    def gather_copy(i, b, d):
        rows = window(i)
        return pltpu.make_async_remote_copy(
            src_ref=c_all.at[core, b, rows, :], dst_ref=c_all.at[core, b, rows, :],
            send_sem=g_send.at[i, d], recv_sem=g_recv.at[i, b],
            device_id=same_core(chip_at(d)), device_id_type=MESH)

    def forward_copy(i, k, b):
        rows = window(i)
        return pltpu.make_async_remote_copy(
            src_ref=c_all.at[k, b, rows, :], dst_ref=c_all.at[k, b, rows, :],
            send_sem=f_send.at[i, b], recv_sem=f_recv.at[i, b],
            device_id=sibling, device_id_type=MESH)

    def final_copy(owner, e):
        here = c_all.at[lax.rem(owner, 2), lax.min(lax.div(owner, 2), blocks - 1), window(last), :]
        return pltpu.make_async_remote_copy(
            src_ref=here, dst_ref=here, send_sem=h_send.at[e], recv_sem=h_recv.at[owner],
            device_id=(pw_at(e), band), device_id_type=MESH)

    def couple(i):
        rows = pl.ds(*pieces[i])
        if i == last:
            value = last_send[core, chip].astype(jnp.float32)
            for e in range(1, n_pw):
                source = pw_at(e)
                pltpu.make_async_remote_copy(
                    src_ref=last_send.at[0, 0], dst_ref=last_recv.at[source],
                    send_sem=l_send.at[e], recv_sem=l_recv.at[source],
                    device_id=(source, band), device_id_type=MESH).wait_recv()
                value += last_recv[source].astype(jnp.float32)
        else:
            value = send[chip, rows, :].astype(jnp.float32)
            for d in range(1, chips):
                source = chip_at(d)
                pltpu.make_async_remote_copy(
                    src_ref=send.at[0, rows, :], dst_ref=recv.at[source, rows, :],
                    send_sem=r_send.at[i, d], recv_sem=r_recv.at[i, source],
                    device_id=same_core(source), device_id_type=MESH).wait_recv()
                value += recv[source, rows, :].astype(jnp.float32)
        total[rows, :] = value
        if windows[i] is None:
            return
        c_all[core, chip, window(i), :] = dot_exact(block[window(i), :], total[...], 0).astype(bf16)
        if i == last:
            for e in range(1, n_pw):
                final_copy(pw, e).start()
        else:
            for d in range(1, chips):
                gather_copy(i, chip, d).start()
            forward_copy(i, core, chip).start()

    def forward(i):
        for d in range(1, chips):
            source = chip_at(d)

            @pl.when(source < blocks)
            def _():
                gather_copy(i, source, d).wait_recv()
                forward_copy(i, core, source).start()

    def out_copy(i):
        rows = window(i)
        return pltpu.make_async_copy(
            c_all.at[:, :, rows, :], c_out.at[:, :, rows, :], out_sem.at[i + 1])

    early = [i for i in range(last) if windows[i] is not None]
    owns = chip < blocks

    own.wait()
    project(0)
    if last > 0:
        sibling_copy(0).start()
        reduce_send(0)
    for i in range(1, last + 1):
        p_copies[i - 1].wait_recv()
        project(i)
        if i < last:
            sibling_copy(i).start()
            reduce_send(i)
    for e in range(1, n_pw):
        pl.when(lax.div(pw_at(e), 2) < blocks)(lambda: last_copy(e).start())

    for i in range(last):
        pl.when(owns)(lambda: couple(i))

    pt[:, :NP] = p_all[0].T
    pt[:, NP:] = p_all[1].T
    pt_copy = pltpu.make_async_copy(pt, pt_out, out_sem.at[0])
    pt_copy.start()

    pl.when(owns)(lambda: couple(last))
    for i in early:
        forward(i)
    for i in early:
        for b in range(blocks):
            forward_copy(i, 1 - core, b).wait_recv()
        out_copy(i).start()
    for copy in p_copies:
        copy.wait_send()
    for i in range(last):
        sibling_copy(i).wait_send()
        for d in range(1, chips):
            pl.when(chip_at(d) < blocks)(lambda: reduce_copy(i, d).wait_send())
    for e in range(1, n_pw):
        pl.when(lax.div(pw_at(e), 2) < blocks)(lambda: last_copy(e).wait_send())

    @pl.when(owns)
    def _():
        for i in early:
            for d in range(1, chips):
                gather_copy(i, chip, d).wait_send()
        for e in range(1, n_pw):
            final_copy(pw, e).wait_send()
    for i in early:
        for b in range(blocks):
            forward_copy(i, core, b).wait_send()
    for e in range(1, n_pw):
        pl.when(lax.div(pw_at(e), 2) < blocks)(lambda: final_copy(pw_at(e), e).wait_recv())
    out_copy(last).start()
    pt_copy.wait()
    for i in early:
        out_copy(i).wait()
    out_copy(last).wait()


def gather_coupled(n_pw, n_band, waves, projectors, coupling, offsets, counts):
    _, depth, columns = waves.shape
    held = projectors.shape[1]
    chips = n_pw // 2
    blocks = columns // LANES
    sizes = pieces_of(n_band, held)
    subs = len(sizes)
    pieces = 1 + (n_band - 1) * subs
    last_rows = sizes[-1]
    bf16, f32 = jnp.bfloat16, jnp.float32
    dma = pltpu.SemaphoreType.DMA
    anywhere = pl.BlockSpec(memory_space=pl.ANY)
    wide = -(-coupling.shape[0] * SLOT // LANES) * LANES
    return pl.pallas_call(
        functools.partial(gather_kernel, n_pw, n_band),
        out_shape=[
            jax.ShapeDtypeStruct((depth, 2 * NP), bf16),
            jax.ShapeDtypeStruct((2, blocks, NP, LANES), bf16),
        ],
        in_specs=[anywhere] * 5,
        out_specs=[anywhere, anywhere],
        scratch_shapes=[
            pltpu.VMEM((2, depth, columns), bf16),
            pltpu.VMEM((2, NP, depth), bf16),
            pltpu.VMEM((2, NP, columns), f32),
            pltpu.VMEM((NP, columns), f32),
            pltpu.VMEM((blocks, NP, LANES), bf16),
            pltpu.VMEM((chips, NP, LANES), bf16),
            pltpu.VMEM((2, blocks, last_rows, LANES), bf16),
            pltpu.VMEM((n_pw, last_rows, LANES), bf16),
            pltpu.VMEM((NP, LANES), f32),
            pltpu.VMEM((2, blocks, NP, LANES), bf16),
            pltpu.VMEM((depth, 2 * NP), bf16),
            pltpu.VMEM((wide, LANES), f32),
            pltpu.VMEM((NP, NP), f32),
            pltpu.VMEM(coupling.shape, f32),
            pltpu.SMEM(offsets.shape, jnp.int32),
            pltpu.SMEM(counts.shape, jnp.int32),
            dma((3,)),
            dma((len(column_tiles(columns)),)), dma((1,)), dma((1 + pieces,)),
            dma((n_band - 1, subs)), dma((n_band - 1, subs)),
            dma((pieces,)), dma((pieces,)),
            dma((pieces, chips)), dma((pieces, chips)),
            dma((n_pw,)), dma((n_pw,)),
            dma((pieces, chips)), dma((pieces, blocks)),
            dma((pieces, blocks)), dma((pieces, blocks)),
            dma((n_pw,)), dma((n_pw,)),
        ],
        compiler_params=pltpu.CompilerParams(
            collective_id=0, has_side_effects=True, vmem_limit_bytes=60 * 2**20),
        name="gather_coupled",
    )(waves, projectors, coupling, offsets, counts)


def row_parts(depth):
    ends = list(range(512, depth, 512)) + [depth]
    return [(first, end - first) for first, end in zip([0] + ends[:-1], ends)]


def spread_kernel(pt, c, out, pt_vmem, c_vmem, rhs, result, in_sem, out_sem):
    blocks = c.shape[1]
    parts = row_parts(pt.shape[0])
    c_copy = pltpu.make_async_copy(c, c_vmem, in_sem.at[0])
    c_copy.start()
    pt_copies = []
    for i, (first, size) in enumerate(parts):
        rows = pl.ds(first, size)
        copy = pltpu.make_async_copy(pt.at[rows, :], pt_vmem.at[rows, :], in_sem.at[i + 1])
        copy.start()
        pt_copies.append(copy)
    c_copy.wait()
    for b in range(blocks):
        c0, c1 = c_vmem[0, b], c_vmem[1, b]
        rhs[b, :NP, :LANES] = c0
        rhs[b, :NP, LANES:] = c1
        rhs[b, NP:, :LANES] = -c1
        rhs[b, NP:, LANES:] = c0
    out_copies = []
    for i, (first, size) in enumerate(parts):
        rows = pl.ds(first, size)
        pt_copies[i].wait()
        for b in range(blocks):
            cols = pl.ds(b * LANES, LANES)
            r = jnp.dot(pt_vmem[rows, :], rhs[b], preferred_element_type=jnp.float32)
            result[0, rows, cols] = r[:, :LANES].astype(result.dtype)
            result[1, rows, cols] = r[:, LANES:].astype(result.dtype)
        for k in range(2):
            copy = pltpu.make_async_copy(
                result.at[k, rows, :], out.at[k, rows, :], out_sem.at[i, k])
            copy.start()
            out_copies.append(copy)
    for copy in out_copies:
        copy.wait()


def spread_back(pt, coupled):
    depth = pt.shape[0]
    blocks = coupled.shape[1]
    parts = len(row_parts(depth))
    bf16 = jnp.bfloat16
    anywhere = pl.BlockSpec(memory_space=pl.ANY)
    return pl.pallas_call(
        spread_kernel,
        out_shape=jax.ShapeDtypeStruct((2, depth, blocks * LANES), bf16),
        in_specs=[anywhere, anywhere],
        out_specs=anywhere,
        scratch_shapes=[
            pltpu.VMEM(pt.shape, bf16),
            pltpu.VMEM(coupled.shape, bf16),
            pltpu.VMEM((blocks, 2 * NP, 2 * LANES), bf16),
            pltpu.VMEM((2, depth, blocks * LANES), bf16),
            pltpu.SemaphoreType.DMA((1 + parts,)),
            pltpu.SemaphoreType.DMA((parts, 2)),
        ],
        compiler_params=pltpu.CompilerParams(vmem_limit_bytes=60 * 2**20),
        name="spread_back",
    )(pt, coupled)


def solution(mesh):
    n_pw, n_band = mesh.shape["pw"], mesh.shape["band"]

    def shards(waves, projectors, coupling, offsets, counts):
        pt, coupled = gather_coupled(n_pw, n_band, waves, projectors, coupling, offsets, counts)
        return spread_back(pt, coupled)

    placed = (P(None, "pw", "band"), P(None, "band", "pw"), P(), P(), P())
    return jax.shard_map(
        shards, mesh=mesh, in_specs=placed, out_specs=P(None, "pw", "band"), check_vma=False
    )
```

```python
import functools

import jax
import jax.numpy as jnp
from jax import lax
from jax.experimental import pallas as pl
from jax.experimental.pallas import tpu as pltpu
from jax.sharding import PartitionSpec as P

NP = 128
M = 13
LANES = 128
SLOT = 16
SHIFT = 4
MESH = pl.DeviceIdType.MESH


def coupling_block(coupling, offsets, counts, spare):
    atoms, most, _ = coupling.shape
    wide = spare.shape[0]
    spare[...] = jnp.zeros_like(spare)
    for a in range(atoms):
        spare[a * SLOT:a * SLOT + most, :most] = coupling[a]

    def iota(shape, dim):
        return lax.broadcasted_iota(jnp.int32, shape, dim)

    place = iota((NP, wide), 1)
    atom, entry = place >> SHIFT, place & (SLOT - 1)
    start = jnp.full((NP, wide), -wide, jnp.int32)
    count = jnp.zeros((NP, wide), jnp.int32)
    for a in range(atoms):
        start = jnp.where(atom == a, offsets[a], start)
        count = jnp.where(atom == a, counts[a], count)
    select = jnp.where((iota((NP, wide), 0) == start + entry) & (entry < count), 1.0, 0.0)
    repeat = jnp.where((iota((LANES, wide), 1) & (SLOT - 1)) == iota((LANES, wide), 0), 1.0, 0.0)
    same = (iota((wide, wide), 0) >> SHIFT) == (iota((wide, wide), 1) >> SHIFT)
    spread = dot_exact(spare[...], repeat, 0)
    spread = jnp.where(same, spread, 0.0)
    raw = dot_exact(dot_exact(select, spread, 0), select, 1)
    return (raw + raw.T) * 0.5


def dot_exact(a, b, dim):
    return lax.dot_general(a, b, (((1,), (dim,)), ((), ())), precision=lax.Precision.HIGHEST,
                           preferred_element_type=jnp.float32)


def column_tiles(columns):
    return [(start, min(256, columns - start)) for start in range(0, columns, 256)]


def pieces_of(n_band, held):
    return [held - SLOT, SLOT] if n_band == 2 and held > SLOT else [held]


def windows_of(n_band, held):
    sizes = pieces_of(n_band, held)
    if n_band != 2 or held <= SLOT:
        return [None] * ((n_band - 1) * len(sizes)) + [(0, NP)]
    ends = [held - SLOT] + [held + sum(sizes[:s + 1]) - SLOT for s in range(len(sizes))]
    ends[-1] = NP
    return [(first, end - first) for first, end in zip([0] + ends[:-1], ends)]


def gather_kernel(n_pw, n_band, waves, proj, coupling_in, offsets_in, counts_in, pt_out, c_out,
                  w, p_all, acc, sib, send, recv, last_send, last_recv, total, c_all, pt, spare, block,
                  coupling, offsets, counts, small_sem, w_sem, own_sem, out_sem, p_send, p_recv, s_send, s_recv,
                  r_send, r_recv, l_send, l_recv, g_send, g_recv, f_send, f_recv, h_send, h_recv):
    pw = lax.axis_index("pw")
    band = lax.axis_index("band")
    chip, core = lax.div(pw, 2), lax.rem(pw, 2)
    chips = n_pw // 2
    held = proj.shape[1]
    columns = waves.shape[2]
    blocks = columns // LANES
    sizes = pieces_of(n_band, held)
    tiles = column_tiles(columns)
    sibling = (chip * 2 + 1 - core, band)
    windows = windows_of(n_band, held)
    bf16 = jnp.bfloat16

    def chip_at(step):
        return lax.rem(chip + step, chips)

    def pw_at(step):
        return lax.rem(pw + step, n_pw)

    def same_core(other):
        return (other * 2 + core, band)

    def sub_row(sender, s):
        if n_band != 2:
            return 0
        first = sum(sizes[:s])
        return pl.multiple_of(first + (1 - sender) * (held - 2 * first - sizes[s]), SLOT)

    def window(i):
        first, size = windows[i]
        if first == 0 and size == NP:
            return pl.ds(0, NP)
        return pl.ds(pl.multiple_of(first + band * (NP - 2 * first - size), SLOT), size)

    own_rows = pl.multiple_of(band * held, held)
    own = pltpu.make_async_copy(proj, p_all.at[:, pl.ds(own_rows, held), :], own_sem.at[0])
    own.start()
    small = [pltpu.make_async_copy(source, target, small_sem.at[i]) for i, (source, target) in enumerate(
        [(coupling_in, coupling), (offsets_in, offsets), (counts_in, counts)])]
    for copy in small:
        copy.start()
    wave_copies = []
    for t, (start, size) in enumerate(tiles):
        copy = pltpu.make_async_copy(
            waves.at[:, :, pl.ds(start, size)], w.at[:, :, pl.ds(start, size)], w_sem.at[t])
        copy.start()
        wave_copies.append(copy)

    barrier = pltpu.get_barrier_semaphore()
    for d in range(1, n_pw):
        pl.semaphore_signal(barrier, inc=1, device_id=(pw_at(d), band), device_id_type=MESH)
    for d in range(1, n_band):
        pl.semaphore_signal(barrier, inc=1, device_id=(pw, lax.rem(band + d, n_band)), device_id_type=MESH)
    for copy in small:
        copy.wait()
    block[...] = coupling_block(coupling, offsets, counts, spare)
    total[...] = jnp.zeros_like(total)
    pl.semaphore_wait(barrier, n_band - 1 + n_pw - 1)

    p_copies = []
    for d in range(1, n_band):
        for s, size in enumerate(sizes):
            row = sub_row(band, s)
            copy = pltpu.make_async_remote_copy(
                src_ref=proj.at[:, pl.ds(row, size), :],
                dst_ref=p_all.at[:, pl.ds(pl.multiple_of(own_rows + row, SLOT), size), :],
                send_sem=p_send.at[d - 1, s], recv_sem=p_recv.at[d - 1, s],
                device_id=(pw, lax.rem(band + d, n_band)), device_id_type=MESH)
            copy.start()
            p_copies.append(copy)

    pieces = [(own_rows, held)]
    for d in range(1, n_band):
        source = lax.rem(band + n_band - d, n_band)
        for s, size in enumerate(sizes):
            pieces.append((pl.multiple_of(source * held + sub_row(source, s), SLOT), size))
    last = len(pieces) - 1
    early = [i for i in range(min(1, last)) if windows[i] is not None]
    direct = [i for i in range(last + 1) if windows[i] is not None and i not in early]

    def project(i):
        row, size = pieces[i]
        rows = pl.ds(row, size)
        p0, p1 = p_all[0, rows, :], p_all[1, rows, :]
        lhs0 = jnp.concatenate([p0, -p1], axis=0)
        lhs1 = jnp.concatenate([p1, p0], axis=0)
        for t, (start, width) in enumerate(tiles):
            if i == 0:
                wave_copies[t].wait()
            cols = pl.ds(start, width)
            r = jnp.dot(lhs0, w[0, :, cols], preferred_element_type=jnp.float32)
            r += jnp.dot(lhs1, w[1, :, cols], preferred_element_type=jnp.float32)
            if i == last:
                for c in range(0, width, LANES):
                    last_send[0, (start + c) // LANES] = r[:size, c:c + LANES].astype(bf16)
                    last_send[1, (start + c) // LANES] = r[size:, c:c + LANES].astype(bf16)
            else:
                acc[0, rows, cols] = r[:size]
                acc[1, rows, cols] = r[size:]

    def sibling_copy(i):
        rows = pl.ds(*pieces[i])
        return pltpu.make_async_remote_copy(
            src_ref=acc.at[1 - core, rows, :], dst_ref=sib.at[rows, :],
            send_sem=s_send.at[i], recv_sem=s_recv.at[i],
            device_id=sibling, device_id_type=MESH)

    def reduce_copy(i, d):
        other = chip_at(d)
        rows = pl.ds(*pieces[i])
        return pltpu.make_async_remote_copy(
            src_ref=send.at[lax.min(other, blocks - 1), rows, :],
            dst_ref=recv.at[chip, rows, :],
            send_sem=r_send.at[i, d], recv_sem=r_recv.at[i, chip],
            device_id=same_core(other), device_id_type=MESH)

    def reduce_send(i):
        rows = pl.ds(*pieces[i])
        sibling_copy(i).wait_recv()
        for b in range(blocks):
            cols = pl.ds(b * LANES, LANES)
            send[b, rows, :] = (acc[core, rows, cols] + sib[rows, cols]).astype(bf16)
        for d in range(1, chips):
            pl.when(chip_at(d) < blocks)(lambda: reduce_copy(i, d).start())

    def last_copy(e):
        target = pw_at(e)
        return pltpu.make_async_remote_copy(
            src_ref=last_send.at[lax.rem(target, 2), lax.min(lax.div(target, 2), blocks - 1)],
            dst_ref=last_recv.at[pw],
            send_sem=l_send.at[e], recv_sem=l_recv.at[pw],
            device_id=(target, band), device_id_type=MESH)

    def gather_copy(i, b, d):
        rows = window(i)
        return pltpu.make_async_remote_copy(
            src_ref=c_all.at[core, b, rows, :], dst_ref=c_all.at[core, b, rows, :],
            send_sem=g_send.at[i, d], recv_sem=g_recv.at[i, b],
            device_id=same_core(chip_at(d)), device_id_type=MESH)

    def forward_copy(i, k, b):
        rows = window(i)
        return pltpu.make_async_remote_copy(
            src_ref=c_all.at[k, b, rows, :], dst_ref=c_all.at[k, b, rows, :],
            send_sem=f_send.at[i, b], recv_sem=f_recv.at[i, b],
            device_id=sibling, device_id_type=MESH)

    def final_copy(i, owner, e):
        here = c_all.at[lax.rem(owner, 2), lax.min(lax.div(owner, 2), blocks - 1), window(i), :]
        return pltpu.make_async_remote_copy(
            src_ref=here, dst_ref=here, send_sem=h_send.at[i, e], recv_sem=h_recv.at[i, owner],
            device_id=(pw_at(e), band), device_id_type=MESH)

    def couple(i):
        rows = pl.ds(*pieces[i])
        if i == last:
            value = last_send[core, chip].astype(jnp.float32)
            for e in range(1, n_pw):
                source = pw_at(e)
                pltpu.make_async_remote_copy(
                    src_ref=last_send.at[0, 0], dst_ref=last_recv.at[source],
                    send_sem=l_send.at[e], recv_sem=l_recv.at[source],
                    device_id=(source, band), device_id_type=MESH).wait_recv()
                value += last_recv[source].astype(jnp.float32)
        else:
            value = send[chip, rows, :].astype(jnp.float32)
            for d in range(1, chips):
                source = chip_at(d)
                pltpu.make_async_remote_copy(
                    src_ref=send.at[0, rows, :], dst_ref=recv.at[source, rows, :],
                    send_sem=r_send.at[i, d], recv_sem=r_recv.at[i, source],
                    device_id=same_core(source), device_id_type=MESH).wait_recv()
                value += recv[source, rows, :].astype(jnp.float32)
        total[rows, :] = value
        if windows[i] is None:
            return
        c_all[core, chip, window(i), :] = dot_exact(block[window(i), :], total[...], 0).astype(bf16)
        if i in direct:
            for e in range(1, n_pw):
                final_copy(i, pw, e).start()
        else:
            for d in range(1, chips):
                gather_copy(i, chip, d).start()
            forward_copy(i, core, chip).start()

    def forward(i):
        for d in range(1, chips):
            source = chip_at(d)

            @pl.when(source < blocks)
            def _():
                gather_copy(i, source, d).wait_recv()
                forward_copy(i, core, source).start()

    def out_copy(i):
        rows = window(i)
        return pltpu.make_async_copy(
            c_all.at[:, :, rows, :], c_out.at[:, :, rows, :], out_sem.at[i + 1])

    owns = chip < blocks

    own.wait()
    project(0)
    if last > 0:
        sibling_copy(0).start()
        reduce_send(0)
    for i in range(1, last + 1):
        p_copies[i - 1].wait_recv()
        project(i)
        if i < last:
            sibling_copy(i).start()
            reduce_send(i)
    for e in range(1, n_pw):
        pl.when(lax.div(pw_at(e), 2) < blocks)(lambda: last_copy(e).start())

    for i in range(last):
        pl.when(owns)(lambda: couple(i))

    pt[:, :NP] = p_all[0].T
    pt[:, NP:] = p_all[1].T
    pt_copy = pltpu.make_async_copy(pt, pt_out, out_sem.at[0])
    pt_copy.start()

    pl.when(owns)(lambda: couple(last))
    for i in early:
        forward(i)
    for i in early:
        for b in range(blocks):
            forward_copy(i, 1 - core, b).wait_recv()
        out_copy(i).start()
    for copy in p_copies:
        copy.wait_send()
    for i in range(last):
        sibling_copy(i).wait_send()
        for d in range(1, chips):
            pl.when(chip_at(d) < blocks)(lambda: reduce_copy(i, d).wait_send())
    for e in range(1, n_pw):
        pl.when(lax.div(pw_at(e), 2) < blocks)(lambda: last_copy(e).wait_send())

    @pl.when(owns)
    def _():
        for i in early:
            for d in range(1, chips):
                gather_copy(i, chip, d).wait_send()
        for e in range(1, n_pw):
            for i in direct:
                final_copy(i, pw, e).wait_send()
    for i in early:
        for b in range(blocks):
            forward_copy(i, core, b).wait_send()
    for i in direct:
        for e in range(1, n_pw):
            pl.when(lax.div(pw_at(e), 2) < blocks)(lambda: final_copy(i, pw_at(e), e).wait_recv())
        out_copy(i).start()
    pt_copy.wait()
    for i in early + direct:
        out_copy(i).wait()


def gather_coupled(n_pw, n_band, waves, projectors, coupling, offsets, counts):
    _, depth, columns = waves.shape
    held = projectors.shape[1]
    chips = n_pw // 2
    blocks = columns // LANES
    sizes = pieces_of(n_band, held)
    subs = len(sizes)
    pieces = 1 + (n_band - 1) * subs
    last_rows = sizes[-1]
    bf16, f32 = jnp.bfloat16, jnp.float32
    dma = pltpu.SemaphoreType.DMA
    anywhere = pl.BlockSpec(memory_space=pl.ANY)
    wide = -(-coupling.shape[0] * SLOT // LANES) * LANES
    return pl.pallas_call(
        functools.partial(gather_kernel, n_pw, n_band),
        out_shape=[
            jax.ShapeDtypeStruct((depth, 2 * NP), bf16),
            jax.ShapeDtypeStruct((2, blocks, NP, LANES), bf16),
        ],
        in_specs=[anywhere] * 5,
        out_specs=[anywhere, anywhere],
        scratch_shapes=[
            pltpu.VMEM((2, depth, columns), bf16),
            pltpu.VMEM((2, NP, depth), bf16),
            pltpu.VMEM((2, NP, columns), f32),
            pltpu.VMEM((NP, columns), f32),
            pltpu.VMEM((blocks, NP, LANES), bf16),
            pltpu.VMEM((chips, NP, LANES), bf16),
            pltpu.VMEM((2, blocks, last_rows, LANES), bf16),
            pltpu.VMEM((n_pw, last_rows, LANES), bf16),
            pltpu.VMEM((NP, LANES), f32),
            pltpu.VMEM((2, blocks, NP, LANES), bf16),
            pltpu.VMEM((depth, 2 * NP), bf16),
            pltpu.VMEM((wide, LANES), f32),
            pltpu.VMEM((NP, NP), f32),
            pltpu.VMEM(coupling.shape, f32),
            pltpu.SMEM(offsets.shape, jnp.int32),
            pltpu.SMEM(counts.shape, jnp.int32),
            dma((3,)),
            dma((len(column_tiles(columns)),)), dma((1,)), dma((1 + pieces,)),
            dma((n_band - 1, subs)), dma((n_band - 1, subs)),
            dma((pieces,)), dma((pieces,)),
            dma((pieces, chips)), dma((pieces, chips)),
            dma((n_pw,)), dma((n_pw,)),
            dma((pieces, chips)), dma((pieces, blocks)),
            dma((pieces, blocks)), dma((pieces, blocks)),
            dma((pieces, n_pw)), dma((pieces, n_pw)),
        ],
        compiler_params=pltpu.CompilerParams(
            collective_id=0, has_side_effects=True, vmem_limit_bytes=60 * 2**20),
        name="gather_coupled",
    )(waves, projectors, coupling, offsets, counts)


def row_parts(depth):
    ends = list(range(512, depth, 512)) + [depth]
    return [(first, end - first) for first, end in zip([0] + ends[:-1], ends)]


def spread_kernel(pt, c, out, pt_vmem, c_vmem, rhs, result, in_sem, out_sem):
    blocks = c.shape[1]
    parts = row_parts(pt.shape[0])
    c_copy = pltpu.make_async_copy(c, c_vmem, in_sem.at[0])
    c_copy.start()
    pt_copies = []
    for i, (first, size) in enumerate(parts):
        rows = pl.ds(first, size)
        copy = pltpu.make_async_copy(pt.at[rows, :], pt_vmem.at[rows, :], in_sem.at[i + 1])
        copy.start()
        pt_copies.append(copy)
    c_copy.wait()
    for b in range(blocks):
        c0, c1 = c_vmem[0, b], c_vmem[1, b]
        rhs[b, :NP, :LANES] = c0
        rhs[b, :NP, LANES:] = c1
        rhs[b, NP:, :LANES] = -c1
        rhs[b, NP:, LANES:] = c0
    out_copies = []
    for i, (first, size) in enumerate(parts):
        rows = pl.ds(first, size)
        pt_copies[i].wait()
        for b in range(blocks):
            cols = pl.ds(b * LANES, LANES)
            r = jnp.dot(pt_vmem[rows, :], rhs[b], preferred_element_type=jnp.float32)
            result[0, rows, cols] = r[:, :LANES].astype(result.dtype)
            result[1, rows, cols] = r[:, LANES:].astype(result.dtype)
        for k in range(2):
            copy = pltpu.make_async_copy(
                result.at[k, rows, :], out.at[k, rows, :], out_sem.at[i, k])
            copy.start()
            out_copies.append(copy)
    for copy in out_copies:
        copy.wait()


def spread_back(pt, coupled):
    depth = pt.shape[0]
    blocks = coupled.shape[1]
    parts = len(row_parts(depth))
    bf16 = jnp.bfloat16
    anywhere = pl.BlockSpec(memory_space=pl.ANY)
    return pl.pallas_call(
        spread_kernel,
        out_shape=jax.ShapeDtypeStruct((2, depth, blocks * LANES), bf16),
        in_specs=[anywhere, anywhere],
        out_specs=anywhere,
        scratch_shapes=[
            pltpu.VMEM(pt.shape, bf16),
            pltpu.VMEM(coupled.shape, bf16),
            pltpu.VMEM((blocks, 2 * NP, 2 * LANES), bf16),
            pltpu.VMEM((2, depth, blocks * LANES), bf16),
            pltpu.SemaphoreType.DMA((1 + parts,)),
            pltpu.SemaphoreType.DMA((parts, 2)),
        ],
        compiler_params=pltpu.CompilerParams(vmem_limit_bytes=60 * 2**20),
        name="spread_back",
    )(pt, coupled)


def solution(mesh):
    n_pw, n_band = mesh.shape["pw"], mesh.shape["band"]

    def shards(waves, projectors, coupling, offsets, counts):
        pt, coupled = gather_coupled(n_pw, n_band, waves, projectors, coupling, offsets, counts)
        return spread_back(pt, coupled)

    placed = (P(None, "pw", "band"), P(None, "band", "pw"), P(), P(), P())
    return jax.shard_map(
        shards, mesh=mesh, in_specs=placed, out_specs=P(None, "pw", "band"), check_vma=False
    )
```
